32 devices in a mesh: region: 8 (over y, x, core), industry: 4 (over z).
Axes of the slice: x: 2, y: 2, z: 4, core: 2. Of those that a mesh axis runs over, the one named last changes fastest.
Arguments:
- position: bfloat16 [8, 1536, 16, 1024], P(None, 'region', None, 'industry'), may hold values from 0.049804688 to 0.94921875
- dual_lower: bfloat16 [8, 1536, 16, 1024], P(None, 'region', None, 'industry'), may hold values from 0.099609375 to 10
- dual_upper: bfloat16 [8, 1536, 16, 1024], P(None, 'region', None, 'industry'), may hold values from 0.099609375 to 10
- upper_bound: int32 [1536, 16, 1024], P('region', None, 'industry'), may hold values from 2 to 63
- suppressed: int32 [1536, 16, 1024], P('region', None, 'industry'), may hold values from 0 to 1
- attack_region: int32 [8], replicated, may hold values from 0 to 1535
- attack_column: int32 [8], replicated, may hold values from 0 to 16383
- dual_row: float32 [8, 1536, 16], P(None, 'region'), may hold values from -3 to 3
- dual_col: float32 [8, 16, 1024], P(None, None, 'industry'), may hold values from -3 to 3
Outputs:
- cell_step: bfloat16 [8, 1536, 16, 1024], P(None, 'region', None, 'industry')
- row_step: float32 [8, 1536, 16], P(None, 'region')
- col_step: float32 [8, 16, 1024], P(None, None, 'industry')
The draws below stay inside these ranges and needn't reach their ends.
All inputs are finite; a program needn't handle non-finite values.
Results may differ from the reference program's by a relative error of at most 0.001.
Values sent between devices are 32-bit elements; how exact they have to be, the bound alone decides.
No kernel may reach another device: no remote copies, remote signals or barrier semaphores. Data moves between devices by JAX's collectives and lax.ppermute only.
A program may use at most 128 MiB of HBM per device.

```python
import math
import jax
import jax.numpy as jnp
from jax import lax

R = 1536
I = 1024
S = 16
K = 8
ITERS = 3


def shuffle_four(sub_key):
    return jax.random.permutation(sub_key, 4)


def block_plan(key):
    plan_key = jax.random.fold_in(key, 40961)
    region_keys = jax.random.split(jax.random.fold_in(plan_key, 1), S)
    industry_keys = jax.random.split(jax.random.fold_in(plan_key, 2), S)
    region_order = jax.vmap(shuffle_four)(region_keys).astype(jnp.int32)
    industry_order = jax.vmap(shuffle_four)(industry_keys).astype(jnp.int32)
    strong_level = jax.random.randint(jax.random.fold_in(plan_key, 3), (S,), 6, 9)
    return (region_order, industry_order, strong_level)


def quarter_signs(block_order, cell_count):
    quarter = jnp.arange(cell_count, dtype=jnp.int32) * 4 // cell_count
    place_rank = block_order[:, quarter].T
    first_sign = 1 - 2 * (place_rank // 2)
    second_sign = 1 - 2 * (place_rank % 2)
    return (first_sign, second_sign)


def draw_suppressed(key, part):
    region_order, industry_order, strong_level = block_plan(key)
    reg_first, reg_second = quarter_signs(region_order, R)
    ind_first, ind_second = quarter_signs(industry_order, I)
    weak_level = 9 - strong_level
    density_level = 10 + strong_level[None, :, None] * reg_first[:, :, None] * ind_first.T[None] + weak_level[None, :, None] * reg_second[:, :, None] * ind_second.T[None]
    ticket = jax.random.randint(jax.random.fold_in(key, 40962), (R, S, I), 0, 20)
    return (ticket < density_level).astype(jnp.int32)


def draw_dual_row(key, part):
    region_order, industry_order, strong_level = block_plan(key)
    reg_first, reg_second = quarter_signs(region_order, R)
    noise_key = jax.random.fold_in(key, 40963)
    first_part = reg_first.astype(jnp.float32)
    second_part = reg_second.astype(jnp.float32)
    noise_part = jnp.clip(0.4 * jax.random.normal(noise_key, (K, R, S), jnp.float32), -1.6, 1.6)
    mean_part = 0.9 * first_part + 0.3 * second_part
    return (mean_part[None] + noise_part).astype(jnp.float32)


def place_ends(drawn, rng, smallest, largest):
    longest = drawn.shape.index(max(drawn.shape))
    spots = []
    for shift in (0, 1):
        where = [jax.random.randint(jax.random.fold_in(rng, axis), (), 0, length) for axis, length in enumerate(drawn.shape)]
        where[longest] = (where[longest] + shift) % drawn.shape[longest]
        spots.append(tuple(where))
    return drawn.at[spots[0]].set(smallest).at[spots[1]].set(largest)


def shard_levels(own_key, dims, cuts, smallest, top_value):
    level, own = 1.0, jax.random.fold_in(own_key, 6)
    for dim, shards_of in cuts:
        steps = jnp.exp(jax.random.uniform(jax.random.fold_in(own, dim), (shards_of,), jnp.float32, smallest / len(cuts), top_value / len(cuts)))
        level = level * jnp.repeat(steps, dims[dim] // shards_of).reshape([-1 if axis == dim else 1 for axis in range(len(dims))])
    return level


def gaussian(key, extent, width, most, pieces=(), kind=jnp.bfloat16):
    result = width * jax.random.normal(key, extent, jnp.float32)
    if pieces:
        result = result * shard_levels(key, extent, pieces, -0.22, 0.18)
    return jnp.clip(result, -most, most).astype(kind)


def setup_inputs(seed: int = 0) -> dict:
    key_list = jax.random.split(jax.random.key(seed), 10)
    position = jnp.clip(0.049804688 + 0.89941406 * jax.random.uniform(key_list[0], (K, R, S, I), jnp.float32) ** shard_levels(key_list[0], (K, R, S, I), ((1, 8), (3, 4)), -0.2, 0.2), 0.049804688, 0.94921875).astype(jnp.bfloat16)
    dual_lower = jnp.clip(jnp.exp(math.log(10.0) - 4.609084 * jax.random.uniform(key_list[1], (K, R, S, I), jnp.float32) ** shard_levels(key_list[1], (K, R, S, I), ((1, 8), (3, 4)), -0.2, 0.2)), 0.099609375, 10.0).astype(jnp.bfloat16)
    dual_upper = jnp.clip(jnp.exp(math.log(10.0) - 4.609084 * jax.random.uniform(key_list[2], (K, R, S, I), jnp.float32) ** shard_levels(key_list[2], (K, R, S, I), ((1, 8), (3, 4)), -0.2, 0.2)), 0.099609375, 10.0).astype(jnp.bfloat16)
    upper_bound = place_ends(jax.random.randint(key_list[3], (R, S, I), 2, 64), jax.random.fold_in(key_list[3], 1), 2, 63).astype(jnp.int32)
    suppressed = draw_suppressed(jax.random.fold_in(key_list[9], 71), 0)
    attack_region = place_ends(jax.random.randint(key_list[5], (K,), 0, R), jax.random.fold_in(key_list[5], 1), 0, R - 1).astype(jnp.int32)
    attack_column = place_ends(jax.random.randint(key_list[6], (K,), 0, S * I), jax.random.fold_in(key_list[6], 1), 0, (S * I) - 1).astype(jnp.int32)
    dual_row = draw_dual_row(jax.random.fold_in(key_list[9], 71), 0)
    dual_col = gaussian(key_list[8], (K, S, I), 0.5, 3.0, ((2, 4),), jnp.float32)
    return {"position": position, "dual_lower": dual_lower, "dual_upper": dual_upper, "upper_bound": upper_bound, "suppressed": suppressed, "attack_region": attack_region, "attack_column": attack_column, "dual_row": dual_row, "dual_col": dual_col}


weight_attack = 8.0
barrier = 0.5
shift_diag = 1.0


def inner_pair(first_row, second_row, first_col, second_col):
    return jnp.sum(first_row * second_row) + jnp.sum(first_col * second_col)


def reference(position, dual_lower, dual_upper, upper_bound, suppressed, attack_region, attack_column, dual_row, dual_col):
    upper = upper_bound.astype(jnp.float32)
    region_ids = jnp.arange(R, dtype=jnp.int32)
    column_ids = jnp.arange(S, dtype=jnp.int32)[:, None] * I + jnp.arange(I, dtype=jnp.int32)[None, :]

    def solve_one(items):
        pos_one, low_one, high_one, region_one, column_one, row_one, col_one = items
        attacked = (region_ids[:, None, None] == region_one) & (column_ids[None] == column_one)
        active = jnp.maximum(suppressed, attacked.astype(jnp.int32)).astype(jnp.float32)
        value = pos_one.astype(jnp.float32) * upper
        slack = upper - value
        scaling = active / (low_one.astype(jnp.float32) / value + high_one.astype(jnp.float32) / slack)
        gradient = jnp.where(attacked, jnp.float32(weight_attack), jnp.float32(0.0)) - row_one[:, :, None] - col_one[None] + barrier * (1.0 / value - 1.0 / slack)
        margin_term = active * (0.5 * upper - value) + scaling * gradient
        res_row = jnp.sum(margin_term, axis=2)
        res_col = jnp.sum(margin_term, axis=0)
        diag_row = jnp.sum(scaling, axis=2) + shift_diag
        diag_col = jnp.sum(scaling, axis=0) + shift_diag

        def couple(part_row, part_col):
            return jnp.sum(scaling * part_col[None], axis=2), jnp.sum(scaling * part_row[:, :, None], axis=0)

        def precondition(vec_row, vec_col):
            base_row, base_col = vec_row / diag_row, vec_col / diag_col
            once_row, once_col = couple(base_row, base_col)
            once_row, once_col = once_row / diag_row, once_col / diag_col
            twice_row, twice_col = couple(once_row, once_col)
            twice_row, twice_col = twice_row / diag_row, twice_col / diag_col
            return base_row - once_row + twice_row, base_col - once_col + twice_col

        pre_row, pre_col = precondition(res_row, res_col)
        dir_row, dir_col = pre_row, pre_col
        rz_now = inner_pair(res_row, pre_row, res_col, pre_col)
        sol_row = jnp.zeros_like(res_row)
        sol_col = jnp.zeros_like(res_col)
        for iteration in range(ITERS):
            image_row, image_col = couple(dir_row, dir_col)
            image_row = diag_row * dir_row + image_row
            image_col = diag_col * dir_col + image_col
            step_len = rz_now / inner_pair(dir_row, image_row, dir_col, image_col)
            sol_row = sol_row + step_len * dir_row
            sol_col = sol_col + step_len * dir_col
            res_row = res_row - step_len * image_row
            res_col = res_col - step_len * image_col
            if iteration + 1 < ITERS:
                pre_row, pre_col = precondition(res_row, res_col)
                rz_next = inner_pair(res_row, pre_row, res_col, pre_col)
                step_ratio = rz_next / rz_now
                dir_row = pre_row + step_ratio * dir_row
                dir_col = pre_col + step_ratio * dir_col
                rz_now = rz_next
        cell_step = (scaling * (sol_row[:, :, None] + sol_col[None] - gradient)).astype(jnp.bfloat16)
        return cell_step, sol_row, sol_col

    return lax.map(solve_one, (position, dual_lower, dual_upper, attack_region, attack_column, dual_row, dual_col))
```

```python
import functools

import jax
import jax.numpy as jnp
from jax import lax
from jax.experimental import pallas as pl
from jax.experimental.pallas import tpu as pltpu
from jax.sharding import PartitionSpec as P

WEIGHT_ATTACK = 8.0
SHIFT_DIAG = 1.0
BLOCK = 8
VMEM_SPEC = pl.BlockSpec(memory_space=pltpu.VMEM)
SMEM_SPEC = pl.BlockSpec(memory_space=pltpu.SMEM)
ANY_SPEC = pl.BlockSpec(memory_space=pl.ANY)
F32 = jnp.float32


def up8(count):
    return -(-count // 8) * 8


def inverse(x):
    rough = pl.reciprocal(x, approx=True)
    return rough * (2.0 - x * rough)


def piece_at(full_ref, index, piece):
    return full_ref[pl.ds(pl.multiple_of(index * piece, 8), piece), :]


def direct(count):
    return count <= 8


def parts(count):
    return count if direct(count) else 1


def put_pieces(full_ref, piece_refs, me, piece):
    count = len(piece_refs)
    if count == 1:
        full_ref[...] = piece_refs[0][...]
        return
    for d, ref in enumerate(piece_refs):
        owner = lax.rem(me + (count - d), count)
        full_ref[pl.ds(pl.multiple_of(owner * piece, 8), piece), :] = ref[...]


def take_pieces(full_refs, piece_refs, me, piece):
    count = len(piece_refs)
    for d, ref in enumerate(piece_refs):
        for j, full in enumerate(full_refs):
            if count == 1:
                ref[:, j] = full[...].reshape(ref.shape[0], ref.shape[2], 128)
            else:
                ref[j] = piece_at(full, lax.rem(me + d, count), piece)


def sweep(scaling_ref, row_ref, col_ref, row_out, col_out, rows, inds):
    col_out[...] = jnp.zeros_like(col_out)
    if row_out.shape[0] > rows:
        row_out[...] = jnp.zeros_like(row_out)

    def step(block, _):
        r0 = pl.multiple_of(block * BLOCK, BLOCK)
        row_wide = jnp.broadcast_to(row_ref[pl.ds(r0, BLOCK), :][:, None, :], (BLOCK, 8, 128))
        row_acc = jnp.zeros((BLOCK, 8, 128), F32)
        for i0 in range(0, inds, 8):
            tile = scaling_ref[pl.ds(r0, BLOCK), i0 : i0 + 8, :]
            row_acc = row_acc + tile * col_ref[i0 : i0 + 8, :][None]
            col_out[i0 : i0 + 8, :] += jnp.sum(tile * row_wide, axis=0)
        row_out[pl.ds(r0, BLOCK), :] = jnp.sum(row_acc, axis=1)
        return 0

    lax.fori_loop(0, rows // BLOCK, step, 0)


def prepare_kernel(
    rows, sizes, inds, probs, nreg, nind, row_piece, col_piece,
    place_ref, flag_ref, region_ref, column_ref,
    pos_hbm, low_hbm, high_hbm, upper_hbm, supp_hbm, drow_ref, dcol_ref,
    *rest,
):
    scaling_ref, barrier_hbm = rest[:2]
    nrow, ncol = parts(nind), parts(nreg)
    row_outs = rest[2 : 2 + nrow]
    col_outs = rest[2 + nrow : 2 + nrow + ncol]
    (tile_s, tile_m, up_s, act_s, row_m, row_s, col_m, col_mt, col_s, col_e) = rest[2 + nrow + ncol :]
    my_reg, my_ind = place_ref[0], place_ref[1]
    half = inds // 128
    col_m[...] = jnp.zeros_like(col_m)
    col_s[...] = jnp.zeros_like(col_s)
    col_e[...] = jnp.zeros_like(col_e)
    row_m[...] = jnp.zeros_like(row_m)
    row_s[...] = jnp.zeros_like(row_s)

    def body(pos_ref, low_ref, high_ref, upper_ref, supp_ref, barrier_ref):
        block = pl.program_id(0)
        r0 = pl.multiple_of(block * BLOCK, BLOCK)
        up_s[...] = upper_ref[...].astype(F32)
        act_s[...] = supp_ref[...].astype(F32)

        def problem(k, _, attacked):
            total = jnp.zeros((sizes, inds), F32)
            for r in range(BLOCK):
                upper = up_s[r]
                active = act_s[r]
                if attacked:
                    own = (region_ref[k] == my_reg * rows + r0 + r).astype(jnp.int32)
                    column = lax.broadcasted_iota(jnp.int32, (sizes, inds), 0) * (inds * nind)
                    column = column + lax.broadcasted_iota(jnp.int32, (sizes, inds), 1) + my_ind * inds
                    hit = column == jnp.where(own == 1, column_ref[k], -1)
                    active = jnp.where(hit, jnp.ones_like(active), active)
                value = pos_ref[k, r].astype(F32) * upper
                slack = upper - value
                den = low_ref[k, r].astype(F32) * slack + high_ref[k, r].astype(F32) * value
                ratio = active * inverse(den)
                scaling = value * slack * ratio
                middle = 0.5 * upper - value
                barrier = middle * ratio
                if attacked:
                    barrier = barrier + jnp.where(hit, WEIGHT_ATTACK * scaling, jnp.zeros_like(scaling))
                margin = middle * active + barrier
                barrier_ref[k, r] = barrier
                place = pl.ds(pl.multiple_of(k * sizes, sizes), sizes)
                tile_s[r, place, :] = scaling
                folded = margin[:, :128]
                for part in range(1, half):
                    folded = folded + margin[:, part * 128 : (part + 1) * 128]
                tile_m[r, place, :] = folded
                total = total + margin
            place = pl.ds(pl.multiple_of(k * sizes, sizes), sizes)
            col_m[place, :] += total
            return 0

        hits = flag_ref[block]

        @pl.when(hits == 0)
        def _():
            lax.fori_loop(0, probs, functools.partial(problem, attacked=False), 0)

        @pl.when(hits != 0)
        def _():
            lax.fori_loop(0, probs, functools.partial(problem, attacked=True), 0)

        def turn(r, _):
            scaling_ref[r0 + r] = tile_s[r].T
            row_m[pl.ds(r0 + r, 1), :] = jnp.sum(tile_m[r].T, axis=0, keepdims=True)
            return 0

        lax.fori_loop(0, BLOCK, turn, 0)

        row_wide = jnp.broadcast_to(drow_ref[pl.ds(r0, BLOCK), :][:, None, :], (BLOCK, 8, 128))
        sum_acc = jnp.zeros((BLOCK, 8, 128), F32)
        dual_acc = jnp.zeros((BLOCK, 8, 128), F32)
        for i0 in range(0, inds, 8):
            tile = scaling_ref[pl.ds(r0, BLOCK), i0 : i0 + 8, :]
            sum_acc = sum_acc + tile
            dual_acc = dual_acc + tile * dcol_ref[i0 : i0 + 8, :][None]
            col_s[i0 : i0 + 8, :] += jnp.sum(tile, axis=0)
            col_e[i0 : i0 + 8, :] += jnp.sum(tile * row_wide, axis=0)
        sums = jnp.sum(sum_acc, axis=1)
        here = pl.ds(r0, BLOCK)
        row_s[here, :] = sums
        row_m[here, :] = row_m[here, :] - drow_ref[here, :] * sums - jnp.sum(dual_acc, axis=1)

    cells = pl.BlockSpec((probs, BLOCK, sizes, inds), lambda b: (0, b, 0, 0))
    shared = pl.BlockSpec((BLOCK, sizes, inds), lambda b: (b, 0, 0))
    pltpu.emit_pipeline(
        body,
        grid=(rows // BLOCK,),
        in_specs=[cells, cells, cells, shared, shared],
        out_specs=[cells],
    )(pos_hbm, low_hbm, high_hbm, upper_hbm, supp_hbm, barrier_hbm)

    if col_mt.shape[0] > inds:
        col_mt[...] = jnp.zeros_like(col_mt)
    col_mt[:inds, :] = col_m[...].T - dcol_ref[:inds, :] * col_s[:inds, :] - col_e[:inds, :]
    take_pieces((row_m, row_s), row_outs, my_ind, row_piece)
    take_pieces((col_mt, col_s), col_outs, my_reg, col_piece)


def couple_kernel(rows, inds, nreg, nind, row_piece, col_piece, place_ref, scaling_ref, *rest):
    nrow, ncol = parts(nind), parts(nreg)
    row_ins, rest = rest[:nrow], rest[nrow:]
    col_ins, rest = rest[:ncol], rest[ncol:]
    row_full, col_full = rest[:2]
    row_outs, rest = rest[2 : 2 + nrow], rest[2 + nrow :]
    col_outs, rest = rest[:ncol], rest[ncol:]
    row_part, col_part = rest
    my_reg, my_ind = place_ref[0], place_ref[1]
    put_pieces(row_full, row_ins, my_ind, row_piece)
    put_pieces(col_full, col_ins, my_reg, col_piece)
    sweep(scaling_ref, row_full, col_full, row_part, col_part, rows, inds)
    take_pieces((row_part,), row_outs, my_ind, row_piece)
    take_pieces((col_part,), col_outs, my_reg, col_piece)


def products_kernel(
    rows, inds, nreg, nind, row_piece, col_piece, iters,
    place_ref, scaling_ref, row_diag_ref, col_diag_ref, *rest,
):
    nrow, ncol = parts(nind), parts(nreg)
    row_ins, rest = rest[:nrow], rest[nrow:]
    col_ins, rest = rest[:ncol], rest[ncol:]
    row_old, rest = rest[:2], rest[2:]
    col_old, rest = rest[:2], rest[2:]
    count = 3 * iters
    row_own, rest = rest[:count], rest[count:]
    col_own, rest = rest[:count], rest[count:]
    out_ref, row_full, col_full, row_z, col_z = rest
    my_reg, my_ind = place_ref[0], place_ref[1]
    put_pieces(row_full, row_ins, my_ind, row_piece)
    put_pieces(col_full, col_ins, my_reg, col_piece)
    row_z[...] = row_old[0][...] - row_old[1][...] + row_full[...]
    col_z[...] = col_old[0][...] - col_old[1][...] + col_full[...]

    def step(block, acc):
        r0 = pl.multiple_of(block * BLOCK, BLOCK)
        row_acc = jnp.zeros((BLOCK, 8, 128), F32)
        for i0 in range(0, inds, 8):
            row_acc = row_acc + scaling_ref[pl.ds(r0, BLOCK), i0 : i0 + 8, :] * col_z[i0 : i0 + 8, :][None]
        return acc + jnp.sum(row_acc, axis=1) * row_z[pl.ds(r0, BLOCK), :]

    cross = lax.fori_loop(0, rows // BLOCK, step, jnp.zeros((BLOCK, 128), F32))
    cross = 2.0 * jnp.sum(cross, axis=0, keepdims=True)

    out_ref[...] = jnp.zeros_like(out_ref)
    row_p = [ref[...] for ref in row_own]
    col_p = [ref[...] for ref in col_own]
    row_zs = [row_p[3 * j] - row_p[3 * j + 1] + row_p[3 * j + 2] for j in range(iters)]
    col_zs = [col_p[3 * j] - col_p[3 * j + 1] + col_p[3 * j + 2] for j in range(iters)]
    slot = 0
    row_diag, col_diag = row_diag_ref[...], col_diag_ref[...]

    def dot(j, row_v, col_v):
        return jnp.sum(row_zs[j] * row_v, axis=0, keepdims=True) + jnp.sum(col_zs[j] * col_v, axis=0, keepdims=True)

    row_first, col_first = row_diag * row_p[0], col_diag * col_p[0]
    for j in range(iters):
        out_ref[slot : slot + 1, :] = dot(j, row_first, col_first)
        slot += 1
    for m in range(iters):
        if m + 1 < iters:
            row_n = row_diag * (row_p[3 * m] + row_p[3 * m + 3])
            col_n = col_diag * (col_p[3 * m] + col_p[3 * m + 3])
        else:
            row_n = row_diag * row_zs[m]
            col_n = col_diag * col_zs[m]
        for j in range(m, iters):
            product = dot(j, row_n, col_n)
            if m + 1 == iters:
                product = product + cross
            out_ref[slot : slot + 1, :] = product
            slot += 1


def ordered_kernel(slot, place_ref, *rest):
    ins, out_ref, slots = rest[:-2], rest[-2], rest[-1]
    ordered_sum(out_ref, ins, slots, place_ref[slot])


def ordered_sum(out_ref, ins, slots, me):
    count = len(ins)
    for d, ref in enumerate(ins):
        slots[lax.rem(me + (count - d), count)] = ref[...]
    total = slots[0]
    for j in range(1, count):
        total = total + slots[j]
    out_ref[...] = total


def finish_kernel(
    rows, sizes, inds, probs, nreg, nind, row_piece, col_piece, iters,
    place_ref, scaling_ref, barrier_hbm, drow_ref, dcol_ref, *rest,
):
    nrow, ncol = parts(nind), parts(nreg)
    sums, rest = rest[:nrow], rest[nrow:]
    row_ins, rest = rest[:nrow], rest[nrow:]
    col_ins, rest = rest[:ncol], rest[ncol:]
    count = 3 * iters - 1
    row_old, rest = rest[:count], rest[count:]
    col_old, rest = rest[:count], rest[count:]
    cell_hbm, row_ref, col_ref, row_full, col_full, row_add, col_add, slots, total_ref = rest
    my_reg, my_ind = place_ref[0], place_ref[1]
    put_pieces(row_full, row_ins, my_ind, row_piece)
    put_pieces(col_full, col_ins, my_reg, col_piece)
    ordered_sum(total_ref, sums, slots, my_ind)
    total = total_ref[...]
    lane = lax.broadcasted_iota(jnp.int32, (128, 128), 0) // sizes
    other = lax.broadcasted_iota(jnp.int32, (128, 128), 1) // sizes
    same = (lane == other).astype(F32)
    total = jnp.dot(total, same, preferred_element_type=F32, precision=lax.Precision.HIGHEST)
    line = [total[j : j + 1, :] for j in range(9)]
    g0, g1, g2, h00, h10, h20, h11, h21, h22 = line
    l1, l2 = h10 / h00, h20 / h00
    d1 = h11 - l1 * h10
    t21 = h21 - l2 * h10
    m21 = t21 / d1
    d2 = h22 - l2 * h20 - m21 * t21
    y1 = g1 - l1 * g0
    y2 = g2 - l2 * g0 - m21 * y1
    c2 = y2 / d2
    c1 = y1 / d1 - m21 * c2
    c0 = g0 / h00 - l1 * c1 - l2 * c2
    coef = (c0, c1, c2)

    def combine(old, last):
        parts = [ref[...] for ref in old] + [last[...]]
        acc = None
        for j in range(iters):
            z = parts[3 * j] - parts[3 * j + 1] + parts[3 * j + 2]
            term = coef[j] * z
            acc = term if acc is None else acc + term
        return acc

    row_y = combine(row_old, row_full)
    col_y = combine(col_old, col_full)
    row_ref[...] = row_y
    col_ref[...] = col_y
    row_add[...] = row_y + drow_ref[...]
    col_add[...] = col_y + dcol_ref[...]

    def body(barrier_ref, cell_ref):
        r0 = pl.program_id(0) * BLOCK

        def one(r, _):
            moved = (col_add[:inds, :] + row_add[pl.ds(r0 + r, 1), :]) * scaling_ref[r0 + r]
            moved = moved.T
            for k in range(probs):
                cell_ref[k, r] = (moved[k * sizes : (k + 1) * sizes, :] - barrier_ref[k, r]).astype(jnp.bfloat16)
            return 0

        lax.fori_loop(0, BLOCK, one, 0)

    cells = pl.BlockSpec((probs, BLOCK, sizes, inds), lambda b: (0, b, 0, 0))
    pltpu.emit_pipeline(
        body, grid=(rows // BLOCK,), in_specs=[cells], out_specs=[cells]
    )(barrier_hbm, cell_hbm)


def shift(x, axis, d, count):
    return lax.ppermute(x, axis, [(j, (j + d) % count) for j in range(count)])


def scatter_sum(pieces, axis, count):
    if not direct(count):
        return lax.psum_scatter(pieces[0], axis, scatter_dimension=0)
    total = pieces[0]
    arrived = [shift(pieces[d], axis, d, count) for d in range(1, count)]
    for part in arrived:
        total = total + part
    return total


def gather(piece, axis, count):
    if not direct(count):
        return [lax.all_gather(piece, axis, tiled=True)]
    return [piece] + [shift(piece, axis, d, count) for d in range(1, count)]


def sum_scalars(part, place, axis, count, slot):
    if not direct(count):
        return lax.psum(part, axis)
    pieces = gather(part, axis, count)
    return pl.pallas_call(
        functools.partial(ordered_kernel, slot),
        out_shape=jax.ShapeDtypeStruct(part.shape, F32),
        in_specs=[SMEM_SPEC] + [VMEM_SPEC] * count,
        out_specs=VMEM_SPEC,
        scratch_shapes=[pltpu.VMEM((count,) + part.shape, F32)],
        compiler_params=pltpu.CompilerParams(vmem_limit_bytes=4 * 1024 * 1024),
        name="regions",
    )(place, *pieces)


def local(
    nreg, nind, iters,
    position, dual_lower, dual_upper, upper_bound, suppressed,
    attack_region, attack_column, dual_row, dual_col,
):
    probs, rows, sizes, inds = position.shape
    row_piece, col_piece = up8(-(-rows // nind)), up8(-(-inds // nreg))
    row_len, col_len = row_piece * nind, col_piece * nreg
    my_reg, my_ind = lax.axis_index("region"), lax.axis_index("industry")
    place = jnp.stack([my_reg, my_ind]).astype(jnp.int32)
    blocks = rows // BLOCK
    first = my_reg * rows + BLOCK * jnp.arange(blocks, dtype=jnp.int32)
    near = (attack_region[None, :] >= first[:, None]) & (attack_region[None, :] < first[:, None] + BLOCK)
    flags = jnp.any(near, axis=1).astype(jnp.int32)
    drow = dual_row.transpose(1, 0, 2).reshape(rows, probs * sizes)
    dcol = dual_col.reshape(probs * sizes, inds).T
    drow = jnp.pad(drow, ((0, row_len - rows), (0, 0)))
    dcol = jnp.pad(dcol, ((0, col_len - inds), (0, 0)))

    def shape(*dims):
        return jax.ShapeDtypeStruct(dims, F32)

    def params(mib):
        return pltpu.CompilerParams(vmem_limit_bytes=mib * 1024 * 1024)

    nrow, ncol = parts(nind), parts(nreg)

    def pieces(count, piece, *inner):
        if direct(count):
            return [shape(*inner, piece, 128)] * count
        return [shape(count, *inner, piece, 128)]

    sizes_all = (rows, inds, nreg, nind, row_piece, col_piece)
    outs = pl.pallas_call(
        functools.partial(prepare_kernel, rows, sizes, inds, probs, nreg, nind, row_piece, col_piece),
        out_shape=[pltpu.VMEM((rows, inds, 128), F32), shape(probs, rows, sizes, inds)]
        + pieces(nind, row_piece, 2)
        + pieces(nreg, col_piece, 2),
        in_specs=[SMEM_SPEC] * 4 + [ANY_SPEC] * 5 + [VMEM_SPEC] * 2,
        out_specs=[VMEM_SPEC, ANY_SPEC] + [VMEM_SPEC] * (nrow + ncol),
        scratch_shapes=[
            pltpu.VMEM((BLOCK, 128, inds), F32),
            pltpu.VMEM((BLOCK, 128, 128), F32),
            pltpu.VMEM((BLOCK, sizes, inds), F32),
            pltpu.VMEM((BLOCK, sizes, inds), F32),
            pltpu.VMEM((row_len, 128), F32),
            pltpu.VMEM((row_len, 128), F32),
            pltpu.VMEM((128, inds), F32),
            pltpu.VMEM((col_len, 128), F32),
            pltpu.VMEM((col_len, 128), F32),
            pltpu.VMEM((col_len, 128), F32),
        ],
        compiler_params=params(14),
        name="prepare",
    )(place, flags, attack_region, attack_column, position, dual_lower, dual_upper, upper_bound, suppressed, drow, dcol)
    scaling, barrier = outs[:2]
    row_pieces, col_pieces = outs[2 : 2 + nrow], outs[2 + nrow :]

    def keep(x):
        return pltpu.with_memory_space_constraint(x, pltpu.VMEM)

    row_both = scatter_sum(row_pieces, "industry", nind)
    col_both = scatter_sum(col_pieces, "region", nreg)
    row_diag, col_diag = row_both[1] + SHIFT_DIAG, col_both[1] + SHIFT_DIAG
    row_now, col_now = row_both[0] / row_diag, col_both[0] / col_diag
    row_own, col_own = [row_now], [col_now]
    row_all, col_all = [], []
    couple = pl.pallas_call(
        functools.partial(couple_kernel, *sizes_all),
        out_shape=[shape(row_len, 128), shape(col_len, 128)]
        + pieces(nind, row_piece, 1)
        + pieces(nreg, col_piece, 1),
        in_specs=[SMEM_SPEC] + [VMEM_SPEC] * (1 + nrow + ncol),
        out_specs=[VMEM_SPEC] * (2 + nrow + ncol),
        scratch_shapes=[pltpu.VMEM((row_len, 128), F32), pltpu.VMEM((col_len, 128), F32)],
        compiler_params=params(8),
        name="couple",
    )
    for _ in range(3 * iters - 1):
        row_in, col_in = gather(row_now, "industry", nind), gather(col_now, "region", nreg)
        outs = couple(place, keep(scaling), *row_in, *col_in)
        row_all.append(outs[0])
        col_all.append(outs[1])
        row_now = scatter_sum(outs[2 : 2 + nrow], "industry", nind)[0] / row_diag
        col_now = scatter_sum(outs[2 + nrow :], "region", nreg)[0] / col_diag
        row_own.append(row_now)
        col_own.append(col_now)
    row_in, col_in = gather(row_now, "industry", nind), gather(col_now, "region", nreg)
    part = pl.pallas_call(
        functools.partial(products_kernel, *sizes_all, iters),
        out_shape=shape(16, 128),
        in_specs=[SMEM_SPEC] + [VMEM_SPEC] * (3 + nrow + ncol + 4 + 6 * iters),
        out_specs=VMEM_SPEC,
        scratch_shapes=[
            pltpu.VMEM((row_len, 128), F32),
            pltpu.VMEM((col_len, 128), F32),
            pltpu.VMEM((row_len, 128), F32),
            pltpu.VMEM((col_len, 128), F32),
        ],
        compiler_params=params(8),
        name="products",
    )(
        place, keep(scaling), row_diag, col_diag, *row_in, *col_in,
        *row_all[-2:], *col_all[-2:], *row_own, *col_own,
    )
    part = sum_scalars(part, place, "region", nreg, 0)
    sums = gather(part, "industry", nind) if direct(nind) else [lax.psum(part, "industry")]
    cell, row_y, col_y = pl.pallas_call(
        functools.partial(finish_kernel, rows, sizes, inds, probs, nreg, nind, row_piece, col_piece, iters),
        out_shape=[
            jax.ShapeDtypeStruct((probs, rows, sizes, inds), jnp.bfloat16),
            shape(row_len, 128),
            shape(col_len, 128),
        ],
        in_specs=[SMEM_SPEC, VMEM_SPEC, ANY_SPEC]
        + [VMEM_SPEC] * (2 + 2 * nrow + ncol + 2 * (3 * iters - 1)),
        out_specs=[ANY_SPEC, VMEM_SPEC, VMEM_SPEC],
        scratch_shapes=[
            pltpu.VMEM((row_len, 128), F32),
            pltpu.VMEM((col_len, 128), F32),
            pltpu.VMEM((row_len, 128), F32),
            pltpu.VMEM((col_len, 128), F32),
            pltpu.VMEM((nind, 16, 128), F32),
            pltpu.VMEM((16, 128), F32),
        ],
        compiler_params=params(12),
        name="finish",
    )(place, keep(scaling), barrier, drow, dcol, *sums, *row_in, *col_in, *row_all, *col_all)
    row_step = row_y[:rows].reshape(rows, probs, sizes).transpose(1, 0, 2)
    col_step = col_y[:inds].T.reshape(probs, sizes, inds)
    return cell, row_step, col_step


def solution(mesh):
    nreg, nind = mesh.shape["region"], mesh.shape["industry"]
    cells = P(None, "region", None, "industry")
    table = P("region", None, "industry")
    row, col = P(None, "region", None), P(None, None, "industry")
    return jax.shard_map(
        functools.partial(local, nreg, nind, 3),
        mesh=mesh,
        in_specs=(cells, cells, cells, table, table, P(), P(), row, col),
        out_specs=(cells, row, col),
        check_vma=False,
    )
```

```python
import functools

import jax
import jax.numpy as jnp
from jax import lax
from jax.experimental import pallas as pl
from jax.experimental.pallas import tpu as pltpu
from jax.sharding import PartitionSpec as P

WEIGHT_ATTACK = 8.0
SHIFT_DIAG = 1.0
BLOCK = 8
LANES = 128
VMEM_MIB = 12
VMEM_SPEC = pl.BlockSpec(memory_space=pltpu.VMEM)
SMEM_SPEC = pl.BlockSpec(memory_space=pltpu.SMEM)
ANY_SPEC = pl.BlockSpec(memory_space=pl.ANY)
F32 = jnp.float32


def shape(*dims):
    return jax.ShapeDtypeStruct(dims, F32)


def params():
    return pltpu.CompilerParams(vmem_limit_bytes=VMEM_MIB * 1024 * 1024)


def inverse(x):
    rough = pl.reciprocal(x, approx=True)
    return rough * (2.0 - x * rough)


def widen(rows):
    return jnp.broadcast_to(rows[:, None, :], (BLOCK, 8, LANES))


def prepare_kernel(
    rows, sizes, inds, probs, nind,
    place_ref, flag_ref, region_ref, column_ref,
    pos_hbm, low_hbm, high_hbm, upper_hbm, supp_hbm, drow_ref, dcol_ref,
    scaling_ref, barrier_hbm, row_ref, col_ref,
    tile_s, tile_m, up_s, act_s, col_m, col_e,
):
    my_reg, my_ind = place_ref[0], place_ref[1]
    blocks = rows // BLOCK
    half = inds // LANES
    col_m[...] = jnp.zeros_like(col_m)
    col_e[...] = jnp.zeros_like(col_e)
    col_ref[...] = jnp.zeros_like(col_ref)

    def turn(slot, before, r):
        scaling_ref[before * BLOCK + r] = tile_s[slot, r].T

    def sums(slot, before):
        r0 = pl.multiple_of(before * BLOCK, BLOCK)
        here = pl.ds(r0, BLOCK)
        drow = drow_ref[here, :]
        row_wide = widen(drow)
        sum_acc = jnp.zeros((BLOCK, 8, LANES), F32)
        dual_acc = jnp.zeros((BLOCK, 8, LANES), F32)
        for i0 in range(0, inds, 8):
            tile = scaling_ref[here, i0 : i0 + 8, :]
            sum_acc = sum_acc + tile
            dual_acc = dual_acc + tile * dcol_ref[i0 : i0 + 8, :][None]
            col_ref[1, i0 : i0 + 8, :] += jnp.sum(tile, axis=0)
            col_e[i0 : i0 + 8, :] += jnp.sum(tile * row_wide, axis=0)
        total = jnp.sum(sum_acc, axis=1)
        margin = lax.dot_general(
            jnp.ones((8, LANES), F32),
            tile_m[slot].reshape(BLOCK * LANES, LANES),
            (((1,), (1,)), ((), ())),
            precision=lax.Precision.HIGHEST,
            preferred_element_type=F32,
        )
        margin = jnp.concatenate([margin[:1, r * LANES : (r + 1) * LANES] for r in range(BLOCK)], axis=0)
        row_ref[1, here, :] = total
        row_ref[0, here, :] = margin - drow * total - jnp.sum(dual_acc, axis=1)

    def body(pos_ref, low_ref, high_ref, upper_ref, supp_ref, barrier_ref):
        block = pl.program_id(0)
        slot = lax.rem(block, 2)
        other = 1 - slot
        before = jnp.maximum(block - 1, 0)
        r0 = block * BLOCK
        up_s[...] = upper_ref[...].astype(F32)
        act_s[...] = supp_ref[...].astype(F32)

        def problem(k, _, attacked):
            turn(other, before, k)
            total = jnp.zeros((sizes, inds), F32)
            place = pl.ds(pl.multiple_of(k * sizes, sizes), sizes)
            for r in range(BLOCK):
                upper = up_s[r]
                active = act_s[r]
                if attacked:
                    own = (region_ref[k] == my_reg * rows + r0 + r).astype(jnp.int32)
                    column = lax.broadcasted_iota(jnp.int32, (sizes, inds), 0) * (inds * nind)
                    column = column + lax.broadcasted_iota(jnp.int32, (sizes, inds), 1) + my_ind * inds
                    hit = column == jnp.where(own == 1, column_ref[k], -1)
                    active = jnp.where(hit, jnp.ones_like(active), active)
                value = pos_ref[k, r].astype(F32) * upper
                slack = upper - value
                den = low_ref[k, r].astype(F32) * slack + high_ref[k, r].astype(F32) * value
                ratio = active * inverse(den)
                scaling = value * slack * ratio
                middle = 0.5 * upper - value
                barrier = middle * ratio
                if attacked:
                    barrier = barrier + jnp.where(hit, WEIGHT_ATTACK * scaling, jnp.zeros_like(scaling))
                margin = middle * active + barrier
                barrier_ref[k, r] = barrier
                tile_s[slot, r, place, :] = scaling
                folded = margin[:, :LANES]
                for part in range(1, half):
                    folded = folded + margin[:, part * LANES : (part + 1) * LANES]
                tile_m[slot, r, place, :] = folded
                total = total + margin
            col_m[place, :] += total
            return 0

        hits = flag_ref[block]

        @pl.when(hits == 0)
        def _():
            lax.fori_loop(0, probs, functools.partial(problem, attacked=False), 0)

        @pl.when(hits != 0)
        def _():
            lax.fori_loop(0, probs, functools.partial(problem, attacked=True), 0)

        @pl.when(block > 0)
        def _():
            sums(other, before)

    cells = pl.BlockSpec((probs, BLOCK, sizes, inds), lambda b: (0, b, 0, 0))
    shared = pl.BlockSpec((BLOCK, sizes, inds), lambda b: (b, 0, 0))
    pltpu.emit_pipeline(
        body, grid=(blocks,), in_specs=[cells, cells, cells, shared, shared], out_specs=[cells]
    )(pos_hbm, low_hbm, high_hbm, upper_hbm, supp_hbm, barrier_hbm)
    last = blocks - 1
    for r in range(BLOCK):
        turn(last % 2, last, r)
    sums(last % 2, last)
    col_ref[0] = col_m[...].T - dcol_ref[...] * col_ref[1] - col_e[...]


def add_up(refs):
    values = [ref[...] for ref in refs]
    while len(values) > 1:
        values = [values[j] + values[j + 1] for j in range(0, len(values), 2)]
    return values[0]


def join_kernel(nrow, ncol, *refs):
    ins, outs = refs[: nrow + ncol], refs[nrow + ncol :]
    outs = list(outs)
    if nrow:
        outs.pop(0)[...] = add_up(ins[:nrow])
    if ncol:
        outs.pop(0)[...] = add_up(ins[nrow:])


def begin_kernel(nrow, ncol, *refs):
    row_diag, col_diag, row_now, col_now = refs[nrow + ncol :]
    for ins, diag, now in ((refs[:nrow], row_diag, row_now), (refs[nrow : nrow + ncol], col_diag, col_now)):
        both = add_up(ins)
        width = both[1] + SHIFT_DIAG
        diag[...] = width
        now[...] = both[0] / width


def couple_kernel(nrow, ncol, scaled, scaling_ref, row_diag, col_diag, *refs):
    row_now, col_now, row_out, col_out = refs[nrow + ncol :]
    rows, inds, _ = scaling_ref.shape
    if scaled:
        row_now[...] = add_up(refs[:nrow]) / row_diag[...]
        col_now[...] = add_up(refs[nrow : nrow + ncol]) / col_diag[...]
    else:
        row_now[...] = refs[0][...]
        col_now[...] = refs[1][...]
    col_out[...] = jnp.zeros_like(col_out)

    def step(block, _):
        here = pl.ds(pl.multiple_of(block * BLOCK, BLOCK), BLOCK)
        row_wide = widen(row_now[here, :])
        acc = jnp.zeros((BLOCK, 8, LANES), F32)
        for i0 in range(0, inds, 8):
            tile = scaling_ref[here, i0 : i0 + 8, :]
            acc = acc + tile * col_now[i0 : i0 + 8, :][None]
            col_out[i0 : i0 + 8, :] += jnp.sum(tile * row_wide, axis=0)
        row_out[here, :] = jnp.sum(acc, axis=1)
        return 0

    lax.fori_loop(0, rows // BLOCK, step, 0)


def products_kernel(iters, nreg, nind, nrow, ncol, scaling_ref, row_diag_ref, col_diag_ref, *rest):
    row_ins, col_ins, rest = rest[:nrow], rest[nrow : nrow + ncol], rest[nrow + ncol :]
    count = 3 * iters - 1
    row_old, col_old = rest[:count], rest[count : 2 * count]
    row_now, col_now, out_ref, row_z, col_z = rest[2 * count :]
    row_now[...] = add_up(row_ins) / row_diag_ref[...]
    col_now[...] = add_up(col_ins) / col_diag_ref[...]
    row_p = [ref[...] for ref in row_old] + [row_now[...]]
    col_p = [ref[...] for ref in col_old] + [col_now[...]]
    rows, inds, _ = scaling_ref.shape
    row_zs = [row_p[3 * j] - row_p[3 * j + 1] + row_p[3 * j + 2] for j in range(iters)]
    col_zs = [col_p[3 * j] - col_p[3 * j + 1] + col_p[3 * j + 2] for j in range(iters)]
    row_z[...] = row_zs[-1]
    col_z[...] = col_zs[-1]

    def step(block, acc):
        here = pl.ds(pl.multiple_of(block * BLOCK, BLOCK), BLOCK)
        part = jnp.zeros((BLOCK, 8, LANES), F32)
        for i0 in range(0, inds, 8):
            part = part + scaling_ref[here, i0 : i0 + 8, :] * col_z[i0 : i0 + 8, :][None]
        return acc + jnp.sum(part, axis=1) * row_z[here, :]

    cross = lax.fori_loop(0, rows // BLOCK, step, jnp.zeros((BLOCK, LANES), F32))
    cross = 2.0 * jnp.sum(cross, axis=0, keepdims=True)
    row_diag, col_diag = row_diag_ref[...], col_diag_ref[...]

    def dot(j, row_v, col_v):
        row_sum = jnp.sum(row_zs[j] * row_v, axis=0, keepdims=True)
        col_sum = jnp.sum(col_zs[j] * col_v, axis=0, keepdims=True)
        return row_sum * (1.0 / nind) + col_sum * (1.0 / nreg)

    out_ref[...] = jnp.zeros_like(out_ref)
    slot = 0
    row_n, col_n = row_diag * row_p[0], col_diag * col_p[0]
    for j in range(iters):
        out_ref[slot : slot + 1, :] = dot(j, row_n, col_n)
        slot += 1
    for m in range(iters):
        last = m + 1 == iters
        row_n = row_diag * (row_zs[m] if last else row_p[3 * m] + row_p[3 * m + 3])
        col_n = col_diag * (col_zs[m] if last else col_p[3 * m] + col_p[3 * m + 3])
        for j in range(m, iters):
            product = dot(j, row_n, col_n)
            out_ref[slot : slot + 1, :] = product + cross if last else product
            slot += 1


def finish_kernel(
    rows, sizes, inds, probs, iters, sums_ref, scaling_ref, barrier_hbm, drow_ref, dcol_ref, *rest
):
    count = 3 * iters
    row_p, col_p = rest[:count], rest[count : 2 * count]
    cell_hbm, row_ref, col_ref, row_add, col_add = rest[2 * count :]
    lane = lax.broadcasted_iota(jnp.int32, (LANES, LANES), 0) // sizes
    other = lax.broadcasted_iota(jnp.int32, (LANES, LANES), 1) // sizes
    same = (lane == other).astype(F32)
    total = jnp.dot(sums_ref[...], same, preferred_element_type=F32, precision=lax.Precision.HIGHEST)
    g0, g1, g2, h00, h10, h20, h11, h21, h22 = [total[j : j + 1, :] for j in range(9)]
    l1, l2 = h10 / h00, h20 / h00
    d1 = h11 - l1 * h10
    t21 = h21 - l2 * h10
    m21 = t21 / d1
    d2 = h22 - l2 * h20 - m21 * t21
    y1 = g1 - l1 * g0
    y2 = g2 - l2 * g0 - m21 * y1
    c2 = y2 / d2
    c1 = y1 / d1 - m21 * c2
    c0 = g0 / h00 - l1 * c1 - l2 * c2

    def combine(refs):
        acc = None
        for j, coef in enumerate((c0, c1, c2)):
            term = coef * (refs[3 * j][...] - refs[3 * j + 1][...] + refs[3 * j + 2][...])
            acc = term if acc is None else acc + term
        return acc

    row_y = combine(row_p)
    col_y = combine(col_p)
    row_ref[...] = row_y
    col_ref[...] = col_y
    row_add[...] = row_y + drow_ref[...]
    col_add[...] = col_y + dcol_ref[...]

    def body(barrier_ref, cell_ref):
        r0 = pl.program_id(0) * BLOCK
        for r in range(BLOCK):
            moved = (col_add[...] + row_add[pl.ds(r0 + r, 1), :]) * scaling_ref[r0 + r]
            moved = moved.T
            for k in range(probs):
                cell_ref[k, r] = (moved[k * sizes : (k + 1) * sizes, :] - barrier_ref[k, r]).astype(jnp.bfloat16)

    cells = pl.BlockSpec((probs, BLOCK, sizes, inds), lambda b: (0, b, 0, 0))
    pltpu.emit_pipeline(body, grid=(rows // BLOCK,), in_specs=[cells], out_specs=[cells])(barrier_hbm, cell_hbm)


def stages(count, most):
    bits = [1 << j for j in range(count.bit_length() - 1)]
    if most == 1:
        return [[bit] for bit in bits]
    return [bits[:1]] + [bits[j : j + most] for j in range(1, len(bits), most)]


def exchange(x, axis, count, bits):
    flips = [0]
    for bit in bits:
        flips = flips + [flip | bit for flip in flips]
    return [x] + [lax.ppermute(x, axis, [(j, j ^ flip) for j in range(count)]) for flip in flips[1:]]


def vmem_call(kernel, outs, name, scratch=()):
    def call(*args):
        return pl.pallas_call(
            kernel,
            out_shape=outs,
            in_specs=[VMEM_SPEC] * len(args),
            out_specs=[VMEM_SPEC] * len(outs),
            scratch_shapes=list(scratch),
            compiler_params=params(),
            name=name,
        )(*args)

    return call


def both_sums(row, col, nreg, nind):
    row_stages, col_stages = stages(nind, 1), stages(nreg, 2)
    row_parts, col_parts = [row], [col]
    for j in range(max(len(row_stages), len(col_stages))):
        with_row, with_col = j < len(row_stages), j < len(col_stages)
        if j:
            ins = (row_parts if with_row else []) + (col_parts if with_col else [])
            outs = [row.shape] * with_row + [col.shape] * with_col
            kernel = functools.partial(
                join_kernel, len(row_parts) if with_row else 0, len(col_parts) if with_col else 0
            )
            summed = list(vmem_call(kernel, [shape(*dims) for dims in outs], "join")(*ins))
            if with_row:
                row = summed.pop(0)
            if with_col:
                col = summed.pop(0)
        if with_row:
            row_parts = exchange(row, "industry", nind, row_stages[j])
        if with_col:
            col_parts = exchange(col, "region", nreg, col_stages[j])
    return row_parts, col_parts


def total_over(x, axis, count):
    for bits in stages(count, 1):
        own, other = exchange(x, axis, count, bits)
        x = own + other
    return x


def local(
    nreg, nind, iters,
    position, dual_lower, dual_upper, upper_bound, suppressed,
    attack_region, attack_column, dual_row, dual_col,
):
    probs, rows, sizes, inds = position.shape
    my_reg, my_ind = lax.axis_index("region"), lax.axis_index("industry")
    place = jnp.stack([my_reg, my_ind]).astype(jnp.int32)
    blocks = rows // BLOCK
    first = my_reg * rows + BLOCK * jnp.arange(blocks, dtype=jnp.int32)
    near = (attack_region[None, :] >= first[:, None]) & (attack_region[None, :] < first[:, None] + BLOCK)
    flags = jnp.any(near, axis=1).astype(jnp.int32)
    drow = dual_row.transpose(1, 0, 2).reshape(rows, LANES)
    dcol = dual_col.reshape(LANES, inds).T

    def in_hbm(x):
        return pltpu.with_memory_space_constraint(x, pltpu.HBM)

    def keep(x):
        return pltpu.with_memory_space_constraint(x, pltpu.VMEM)

    scaling, barrier, row_both, col_both = pl.pallas_call(
        functools.partial(prepare_kernel, rows, sizes, inds, probs, nind),
        out_shape=[
            pltpu.VMEM((rows, inds, LANES), F32),
            shape(probs, rows, sizes, inds),
            shape(2, rows, LANES),
            shape(2, inds, LANES),
        ],
        in_specs=[SMEM_SPEC] * 4 + [ANY_SPEC] * 5 + [VMEM_SPEC] * 2,
        out_specs=[VMEM_SPEC, ANY_SPEC, VMEM_SPEC, VMEM_SPEC],
        scratch_shapes=[
            pltpu.VMEM((2, BLOCK, LANES, inds), F32),
            pltpu.VMEM((2, BLOCK, LANES, LANES), F32),
            pltpu.VMEM((BLOCK, sizes, inds), F32),
            pltpu.VMEM((BLOCK, sizes, inds), F32),
            pltpu.VMEM((LANES, inds), F32),
            pltpu.VMEM((inds, LANES), F32),
        ],
        compiler_params=params(),
        name="prepare",
    )(
        place, flags, attack_region, attack_column,
        *map(in_hbm, (position, dual_lower, dual_upper, upper_bound, suppressed)), drow, dcol,
    )
    scaling = keep(scaling)
    margins = [shape(rows, LANES), shape(inds, LANES)]
    row_parts, col_parts = both_sums(row_both, col_both, nreg, nind)
    kernel = functools.partial(begin_kernel, len(row_parts), len(col_parts))
    row_diag, col_diag, row_now, col_now = vmem_call(kernel, margins * 2, "begin")(*row_parts, *col_parts)
    row_parts, col_parts = [row_now], [col_now]
    row_p, col_p = [], []
    for j in range(3 * iters - 1):
        kernel = functools.partial(couple_kernel, len(row_parts), len(col_parts), j > 0)
        row_now, col_now, row_out, col_out = vmem_call(kernel, margins * 2, "couple")(
            scaling, row_diag, col_diag, *row_parts, *col_parts
        )
        row_p.append(row_now)
        col_p.append(col_now)
        row_parts, col_parts = both_sums(row_out, col_out, nreg, nind)
    kernel = functools.partial(products_kernel, iters, nreg, nind, len(row_parts), len(col_parts))
    scratch = [pltpu.VMEM((rows, LANES), F32), pltpu.VMEM((inds, LANES), F32)]
    row_now, col_now, part = vmem_call(kernel, margins + [shape(16, LANES)], "products", scratch)(
        scaling, row_diag, col_diag, *row_parts, *col_parts, *row_p, *col_p
    )
    row_p.append(row_now)
    col_p.append(col_now)
    sums = total_over(total_over(part, "region", nreg), "industry", nind)
    cell, row_y, col_y = pl.pallas_call(
        functools.partial(finish_kernel, rows, sizes, inds, probs, iters),
        out_shape=[
            jax.ShapeDtypeStruct((probs, rows, sizes, inds), jnp.bfloat16),
            shape(rows, LANES),
            shape(inds, LANES),
        ],
        in_specs=[VMEM_SPEC] * 2 + [ANY_SPEC] + [VMEM_SPEC] * (2 + 6 * iters),
        out_specs=[ANY_SPEC, VMEM_SPEC, VMEM_SPEC],
        scratch_shapes=[pltpu.VMEM((rows, LANES), F32), pltpu.VMEM((inds, LANES), F32)],
        compiler_params=params(),
        name="finish",
    )(sums, scaling, barrier, drow, dcol, *row_p, *col_p)
    row_step = row_y.reshape(rows, probs, sizes).transpose(1, 0, 2)
    col_step = col_y.T.reshape(probs, sizes, inds)
    return cell, row_step, col_step


def solution(mesh):
    nreg, nind = mesh.shape["region"], mesh.shape["industry"]
    cells = P(None, "region", None, "industry")
    table = P("region", None, "industry")
    row, col = P(None, "region", None), P(None, None, "industry")
    return jax.shard_map(
        functools.partial(local, nreg, nind, 3),
        mesh=mesh,
        in_specs=(cells, cells, cells, table, table, P(), P(), row, col),
        out_specs=(cells, row, col),
        check_vma=False,
    )
```

```python
import functools

import jax
import jax.numpy as jnp
from jax import lax
from jax.experimental import pallas as pl
from jax.experimental.pallas import tpu as pltpu
from jax.sharding import PartitionSpec as P

WEIGHT_ATTACK = 8.0
SHIFT_DIAG = 1.0
BLOCK = 8
LANES = 128
VMEM_MIB = 12
RATIO_IN_VMEM = False
VMEM_SPEC = pl.BlockSpec(memory_space=pltpu.VMEM)
SMEM_SPEC = pl.BlockSpec(memory_space=pltpu.SMEM)
ANY_SPEC = pl.BlockSpec(memory_space=pl.ANY)
F32 = jnp.float32


def shape(*dims):
    return jax.ShapeDtypeStruct(dims, F32)


def params():
    return pltpu.CompilerParams(vmem_limit_bytes=VMEM_MIB * 1024 * 1024)


def inverse(x):
    rough = pl.reciprocal(x, approx=True)
    return rough * (2.0 - x * rough)


def widen(rows):
    return jnp.broadcast_to(rows[:, None, :], (BLOCK, 8, LANES))


def attacked_tile(info_ref, k, row, sizes, inds, nind):
    probs = (info_ref.shape[0] - 2) // 2
    first = info_ref[1] * inds
    column = lax.broadcasted_iota(jnp.int32, (sizes, inds), 0) * (inds * nind)
    column = column + lax.broadcasted_iota(jnp.int32, (sizes, inds), 1) + first
    return column == jnp.where(info_ref[2 + k] == row, info_ref[2 + probs + k], -1)


def any_attack(info_ref, first_row):
    probs = (info_ref.shape[0] - 2) // 2
    hits = jnp.int32(0)
    for k in range(probs):
        offset = info_ref[2 + k] - first_row
        hits = hits + jnp.where((offset >= 0) & (offset < BLOCK), 1, 0)
    return hits


def split_halves(full, keep_ref, send_ref, core):
    half = full.shape[-2] // 2
    for ref, which in ((keep_ref, core), (send_ref, 1 - core)):
        ref[...] = full[..., pl.ds(pl.multiple_of(which * half, 8), half), :]


def prepare_kernel(
    rows, sizes, inds, probs, nind,
    info_ref, pos_hbm, low_hbm, high_hbm, upper_hbm, supp_hbm, drow_ref, dcol_ref,
    scaling_ref, ratio_ref, row_ref, keep_ref, send_ref,
    tile_s, tile_m, up_s, act_s, col_m, col_e, drow_t, dcol_t, col_ref,
):
    blocks = rows // BLOCK
    half = inds // LANES
    first_row = info_ref[0] * rows
    col_m[...] = jnp.zeros_like(col_m)
    col_e[...] = jnp.zeros_like(col_e)
    col_ref[...] = jnp.zeros_like(col_ref)
    drow_t[...] = drow_ref[...].T
    dcol_t[...] = dcol_ref[...].T

    def turn(slot, before, r):
        scaling_ref[before * BLOCK + r] = tile_s[slot, r].T

    def sums(slot, before):
        r0 = pl.multiple_of(before * BLOCK, BLOCK)
        here = pl.ds(r0, BLOCK)
        drow = drow_t[here, :]
        row_wide = widen(drow)
        sum_acc = jnp.zeros((BLOCK, 8, LANES), F32)
        dual_acc = jnp.zeros((BLOCK, 8, LANES), F32)
        for i0 in range(0, inds, 8):
            tile = scaling_ref[here, i0 : i0 + 8, :]
            sum_acc = sum_acc + tile
            dual_acc = dual_acc + tile * dcol_t[i0 : i0 + 8, :][None]
            col_ref[1, i0 : i0 + 8, :] += jnp.sum(tile, axis=0)
            col_e[i0 : i0 + 8, :] += jnp.sum(tile * row_wide, axis=0)
        total = jnp.sum(sum_acc, axis=1)
        margin = lax.dot_general(
            jnp.ones((8, LANES), F32),
            tile_m[slot].reshape(BLOCK * LANES, LANES),
            (((1,), (1,)), ((), ())),
            precision=lax.Precision.HIGHEST,
            preferred_element_type=F32,
        )
        margin = jnp.concatenate([margin[:1, r * LANES : (r + 1) * LANES] for r in range(BLOCK)], axis=0)
        row_ref[1, here, :] = total
        row_ref[0, here, :] = margin - drow * total - jnp.sum(dual_acc, axis=1)

    def body(pos_ref, low_ref, high_ref, upper_ref, supp_ref, *ratio_out):
        block = pl.program_id(0)
        slot = lax.rem(block, 2)
        other = 1 - slot
        before = jnp.maximum(block - 1, 0)
        r0 = block * BLOCK
        up_s[...] = upper_ref[...].astype(F32)
        act_s[...] = supp_ref[...].astype(F32)

        def problem(k, _, attacked):
            turn(other, before, k)
            total = jnp.zeros((sizes, inds), F32)
            place = pl.ds(pl.multiple_of(k * sizes, sizes), sizes)
            for r in range(BLOCK):
                upper = up_s[r]
                active = act_s[r]
                if attacked:
                    hit = attacked_tile(info_ref, k, first_row + r0 + r, sizes, inds, nind)
                    active = jnp.where(hit, jnp.ones_like(active), active)
                value = pos_ref[k, r].astype(F32) * upper
                slack = upper - value
                den = low_ref[k, r].astype(F32) * slack + high_ref[k, r].astype(F32) * value
                ratio = active * inverse(den)
                scaling = value * slack * ratio
                middle = 0.5 * upper - value
                margin = middle * (active + ratio)
                if attacked:
                    margin = margin + jnp.where(hit, WEIGHT_ATTACK * scaling, jnp.zeros_like(scaling))
                if ratio_out:
                    ratio_out[0][k, r] = ratio
                else:
                    ratio_ref[k, r0 + r] = ratio
                tile_s[slot, r, place, :] = scaling
                folded = margin[:, :LANES]
                for part in range(1, half):
                    folded = folded + margin[:, part * LANES : (part + 1) * LANES]
                tile_m[slot, r, place, :] = folded
                total = total + margin
            col_m[place, :] += total
            return 0

        hits = any_attack(info_ref, first_row + r0)

        @pl.when(hits == 0)
        def _():
            lax.fori_loop(0, probs, functools.partial(problem, attacked=False), 0)

        @pl.when(hits != 0)
        def _():
            lax.fori_loop(0, probs, functools.partial(problem, attacked=True), 0)

        @pl.when(block > 0)
        def _():
            sums(other, before)

    cells = pl.BlockSpec((probs, BLOCK, sizes, inds), lambda b: (0, b, 0, 0))
    shared = pl.BlockSpec((BLOCK, sizes, inds), lambda b: (b, 0, 0))
    pltpu.emit_pipeline(
        body,
        grid=(blocks,),
        in_specs=[cells, cells, cells, shared, shared],
        out_specs=[] if RATIO_IN_VMEM else [cells],
    )(pos_hbm, low_hbm, high_hbm, upper_hbm, supp_hbm, *([] if RATIO_IN_VMEM else [ratio_ref]))
    last = blocks - 1
    for r in range(BLOCK):
        turn(last % 2, last, r)
    sums(last % 2, last)
    col_ref[0] = col_m[...].T - dcol_t[...] * col_ref[1] - col_e[...]
    split_halves(col_ref, keep_ref, send_ref, lax.rem(info_ref[0], 2))


def add_up(refs):
    values = [ref[...] for ref in refs]
    while len(values) > 1:
        values = [values[j] + values[j + 1] for j in range(0, len(values), 2)]
    return values[0]


def join_kernel(*refs):
    refs[-1][...] = add_up(refs[:-1])


def begin_kernel(count, info_ref, *refs):
    own, other, row_diag, col_diag, row_now, col_now = refs[count:]
    both = add_up(refs[:count])
    row_diag[...] = both[1] + SHIFT_DIAG
    row_now[...] = both[0] / row_diag[...]
    half = own.shape[1]
    core = lax.rem(info_ref[0], 2)
    for ref, which in ((own, core), (other, 1 - core)):
        here = pl.ds(pl.multiple_of(which * half, 8), half)
        width = ref[1] + SHIFT_DIAG
        col_diag[here, :] = width
        col_now[here, :] = ref[0] / width


def row_end_kernel(*refs):
    refs[-1][...] = add_up(refs[:-2]) / refs[-2][...]


def join_halves(info_ref, own, other, diag, out):
    half = own.shape[0]
    core = lax.rem(info_ref[0], 2)
    for ref, which in ((own, core), (other, 1 - core)):
        here = pl.ds(pl.multiple_of(which * half, 8), half)
        out[here, :] = ref[...] / diag[here, :]


def row_kernel(scaling_ref, col_ref, out_ref):
    rows, inds, _ = scaling_ref.shape

    def step(block, _):
        here = pl.ds(pl.multiple_of(block * BLOCK, BLOCK), BLOCK)
        acc = jnp.zeros((BLOCK, 8, LANES), F32)
        for i0 in range(0, inds, 8):
            acc = acc + scaling_ref[here, i0 : i0 + 8, :] * col_ref[i0 : i0 + 8, :][None]
        out_ref[here, :] = jnp.sum(acc, axis=1)
        return 0

    lax.fori_loop(0, rows // BLOCK, step, 0)


def col_kernel(info_ref, scaling_ref, row_ref, _, keep_ref, send_ref, out_ref):
    rows, inds, _ = scaling_ref.shape
    out_ref[...] = jnp.zeros_like(out_ref)

    def step(block, _):
        here = pl.ds(pl.multiple_of(block * BLOCK, BLOCK), BLOCK)
        row_wide = widen(row_ref[here, :])
        for i0 in range(0, inds, 8):
            out_ref[i0 : i0 + 8, :] += jnp.sum(scaling_ref[here, i0 : i0 + 8, :] * row_wide, axis=0)
        return 0

    lax.fori_loop(0, rows // BLOCK, step, 0)
    split_halves(out_ref, keep_ref, send_ref, lax.rem(info_ref[0], 2))


def products_kernel(iters, nreg, nind, scaling_ref, row_diag_ref, col_diag_ref, *rest):
    count = 3 * iters
    row_p, col_p = [ref[...] for ref in rest[:count]], [ref[...] for ref in rest[count : 2 * count]]
    out_ref, row_z, col_z = rest[2 * count :]
    rows, inds, _ = scaling_ref.shape
    row_zs = [row_p[3 * j] - row_p[3 * j + 1] + row_p[3 * j + 2] for j in range(iters)]
    col_zs = [col_p[3 * j] - col_p[3 * j + 1] + col_p[3 * j + 2] for j in range(iters)]
    row_z[...] = row_zs[-1]
    col_z[...] = col_zs[-1]

    def step(block, acc):
        here = pl.ds(pl.multiple_of(block * BLOCK, BLOCK), BLOCK)
        part = jnp.zeros((BLOCK, 8, LANES), F32)
        for i0 in range(0, inds, 8):
            part = part + scaling_ref[here, i0 : i0 + 8, :] * col_z[i0 : i0 + 8, :][None]
        return acc + jnp.sum(part, axis=1) * row_z[here, :]

    cross = lax.fori_loop(0, rows // BLOCK, step, jnp.zeros((BLOCK, LANES), F32))
    cross = 2.0 * jnp.sum(cross, axis=0, keepdims=True)
    row_diag, col_diag = row_diag_ref[...], col_diag_ref[...]

    def dot(j, row_v, col_v):
        row_sum = jnp.sum(row_zs[j] * row_v, axis=0, keepdims=True)
        col_sum = jnp.sum(col_zs[j] * col_v, axis=0, keepdims=True)
        return row_sum * (1.0 / nind) + col_sum * (1.0 / nreg)

    out_ref[...] = jnp.zeros_like(out_ref)
    slot = 0
    row_n, col_n = row_diag * row_p[0], col_diag * col_p[0]
    for j in range(iters):
        out_ref[slot : slot + 1, :] = dot(j, row_n, col_n)
        slot += 1
    for m in range(iters):
        last = m + 1 == iters
        row_n = row_diag * (row_zs[m] if last else row_p[3 * m] + row_p[3 * m + 3])
        col_n = col_diag * (col_zs[m] if last else col_p[3 * m] + col_p[3 * m + 3])
        for j in range(m, iters):
            product = dot(j, row_n, col_n)
            out_ref[slot : slot + 1, :] = product + cross if last else product
            slot += 1


def finish_kernel(
    rows, sizes, inds, probs, nind, iters, nsum,
    info_ref, pos_hbm, upper_hbm, ratio_ref, drow_ref, dcol_ref, *rest,
):
    count = 3 * iters
    sums, rest = rest[:nsum], rest[nsum:]
    row_p, col_p = rest[:count], rest[count : 2 * count]
    cell_hbm, row_ref, col_ref, row_add, col_add, up_s, row_s = rest[2 * count :]
    first_row = info_ref[0] * rows
    lane = lax.broadcasted_iota(jnp.int32, (LANES, LANES), 0) // sizes
    other = lax.broadcasted_iota(jnp.int32, (LANES, LANES), 1) // sizes
    same = (lane == other).astype(F32)
    total = jnp.dot(add_up(sums), same, preferred_element_type=F32, precision=lax.Precision.HIGHEST)
    g0, g1, g2, h00, h10, h20, h11, h21, h22 = [total[j : j + 1, :] for j in range(9)]
    l1, l2 = h10 / h00, h20 / h00
    d1 = h11 - l1 * h10
    t21 = h21 - l2 * h10
    m21 = t21 / d1
    d2 = h22 - l2 * h20 - m21 * t21
    y1 = g1 - l1 * g0
    y2 = g2 - l2 * g0 - m21 * y1
    c2 = y2 / d2
    c1 = y1 / d1 - m21 * c2
    c0 = g0 / h00 - l1 * c1 - l2 * c2

    def combine(refs):
        acc = None
        for j, coef in enumerate((c0, c1, c2)):
            term = coef * (refs[3 * j][...] - refs[3 * j + 1][...] + refs[3 * j + 2][...])
            acc = term if acc is None else acc + term
        return acc

    row_y = combine(row_p)
    col_turned = combine(col_p).T
    row_ref[...] = row_y.T
    col_ref[...] = col_turned
    row_add[...] = row_y + drow_ref[...].T
    col_add[...] = col_turned + dcol_ref[...]

    def body(pos_ref, upper_ref, *refs):
        cell_ref = refs[-1]
        r0 = pl.multiple_of(pl.program_id(0) * BLOCK, BLOCK)
        up_s[...] = upper_ref[...].astype(F32)
        row_s[...] = row_add[pl.ds(r0, BLOCK), :].T

        def problem(k, _, attacked):
            place = pl.ds(pl.multiple_of(k * sizes, sizes), sizes)
            for r in range(BLOCK):
                upper = up_s[r]
                value = pos_ref[k, r].astype(F32) * upper
                total = row_s[place, r : r + 1] + col_add[place, :]
                if attacked:
                    hit = attacked_tile(info_ref, k, first_row + r0 + r, sizes, inds, nind)
                    total = jnp.where(hit, total - WEIGHT_ATTACK, total)
                ratio = refs[0][k, r] if len(refs) > 1 else ratio_ref[k, r0 + r]
                cell = ratio * (value * (upper - value) * total - (0.5 * upper - value))
                cell_ref[k, r] = cell.astype(jnp.bfloat16)
            return 0

        hits = any_attack(info_ref, first_row + r0)

        @pl.when(hits == 0)
        def _():
            lax.fori_loop(0, probs, functools.partial(problem, attacked=False), 0)

        @pl.when(hits != 0)
        def _():
            lax.fori_loop(0, probs, functools.partial(problem, attacked=True), 0)

    cells = pl.BlockSpec((probs, BLOCK, sizes, inds), lambda b: (0, b, 0, 0))
    shared = pl.BlockSpec((BLOCK, sizes, inds), lambda b: (b, 0, 0))
    more = [] if RATIO_IN_VMEM else [ratio_ref]
    pltpu.emit_pipeline(
        body, grid=(rows // BLOCK,), in_specs=[cells, shared] + [cells] * len(more), out_specs=[cells]
    )(pos_hbm, upper_hbm, *more, cell_hbm)


def bits_of(count):
    return [1 << j for j in range(count.bit_length() - 1)]


def exchange(x, axis, count, bits):
    flips = [0]
    for bit in bits:
        flips = flips + [flip | bit for flip in flips]
    return [x] + [lax.ppermute(x, axis, [(j, j ^ flip) for j in range(count)]) for flip in flips[1:]]


def vmem_call(kernel, outs, name, scratch=(), cost=None, scalars=0):
    def call(*args):
        return pl.pallas_call(
            kernel,
            out_shape=outs,
            in_specs=[SMEM_SPEC] * scalars + [VMEM_SPEC] * (len(args) - scalars),
            out_specs=[VMEM_SPEC] * len(outs),
            scratch_shapes=list(scratch),
            compiler_params=params(),
            cost_estimate=cost,
            name=name,
        )(*args)

    return call


def join(parts):
    return vmem_call(join_kernel, [shape(*parts[0].shape)], "join")(*parts)[0]


def row_sum(x, nind):
    parts = [x]
    for bit in bits_of(nind):
        if len(parts) > 1:
            x = join(parts)
        parts = exchange(x, "industry", nind, [bit])
    return parts


def col_sum(keep, send, nreg):
    (arrived,) = exchange(send, "region", nreg, [1])[1:]
    x = join([keep, arrived])
    bits = bits_of(nreg)[1:]
    for j in range(0, len(bits), 2):
        x = join(exchange(x, "region", nreg, bits[j : j + 2]))
    return exchange(x, "region", nreg, [1])


def local(
    nreg, nind, iters,
    position, dual_lower, dual_upper, upper_bound, suppressed,
    attack_region, attack_column, dual_row, dual_col,
):
    probs, rows, sizes, inds = position.shape
    my_reg, my_ind = lax.axis_index("region"), lax.axis_index("industry")
    info = jnp.concatenate([jnp.stack([my_reg, my_ind]).astype(jnp.int32), attack_region, attack_column])
    drow = dual_row.transpose(0, 2, 1).reshape(LANES, rows)
    dcol = dual_col.reshape(LANES, inds)
    half = inds // 2

    def in_hbm(x):
        return pltpu.with_memory_space_constraint(x, pltpu.HBM)

    def keep(x):
        return pltpu.with_memory_space_constraint(x, pltpu.VMEM)

    position, dual_lower, dual_upper = map(in_hbm, (position, dual_lower, dual_upper))
    upper_bound, suppressed = map(in_hbm, (upper_bound, suppressed))
    whole = (probs, rows, sizes, inds)
    scaling, ratio, row_both, col_keep, col_send = pl.pallas_call(
        functools.partial(prepare_kernel, rows, sizes, inds, probs, nind),
        out_shape=[
            pltpu.VMEM((rows, inds, LANES), F32),
            pltpu.VMEM(whole, F32) if RATIO_IN_VMEM else shape(*whole),
            shape(2, rows, LANES),
            shape(2, half, LANES),
            shape(2, half, LANES),
        ],
        in_specs=[SMEM_SPEC] + [ANY_SPEC] * 5 + [VMEM_SPEC] * 2,
        out_specs=[VMEM_SPEC, VMEM_SPEC if RATIO_IN_VMEM else ANY_SPEC] + [VMEM_SPEC] * 3,
        scratch_shapes=[
            pltpu.VMEM((2, BLOCK, LANES, inds), F32),
            pltpu.VMEM((2, BLOCK, LANES, LANES), F32),
            pltpu.VMEM((BLOCK, sizes, inds), F32),
            pltpu.VMEM((BLOCK, sizes, inds), F32),
            pltpu.VMEM((LANES, inds), F32),
            pltpu.VMEM((inds, LANES), F32),
            pltpu.VMEM((rows, LANES), F32),
            pltpu.VMEM((inds, LANES), F32),
            pltpu.VMEM((2, inds, LANES), F32),
        ],
        compiler_params=params(),
        name="prepare",
    )(info, position, dual_lower, dual_upper, upper_bound, suppressed, drow, dcol)
    scaling = keep(scaling)
    if RATIO_IN_VMEM:
        ratio = keep(ratio)
    cells = rows * inds * LANES
    cost = pl.CostEstimate(flops=2 * cells, bytes_accessed=4 * cells, transcendentals=0)
    margins = [shape(rows, LANES), shape(inds, LANES)]
    row_parts = row_sum(row_both, nind)
    col_halves = col_sum(col_keep, col_send, nreg)
    kernel = functools.partial(begin_kernel, len(row_parts))
    row_diag, col_diag, row_now, col_now = vmem_call(kernel, margins * 2, "begin", scalars=1)(
        info, *row_parts, *col_halves
    )
    row_p, col_p = [row_now], [col_now]
    for _ in range(3 * iters - 1):
        (row_out,) = vmem_call(row_kernel, margins[:1], "row_sweep", cost=cost)(scaling, col_p[-1])
        col_keep, col_send = vmem_call(
            col_kernel, [shape(half, LANES)] * 2, "col_sweep", [pltpu.VMEM((inds, LANES), F32)], cost, 1
        )(info, scaling, row_p[-1], row_out)
        row_parts = row_sum(row_out, nind)
        col_halves = col_sum(col_keep, col_send, nreg)
        row_p += vmem_call(row_end_kernel, margins[:1], "row_end")(*row_parts, row_diag)
        col_p += vmem_call(join_halves, margins[1:], "col_end", scalars=1)(info, *col_halves, col_diag)
    kernel = functools.partial(products_kernel, iters, nreg, nind)
    scratch = [pltpu.VMEM((rows, LANES), F32), pltpu.VMEM((inds, LANES), F32)]
    (part,) = vmem_call(kernel, [shape(16, LANES)], "products", scratch)(
        scaling, row_diag, col_diag, *row_p, *col_p
    )
    bits = bits_of(nreg)
    part = join(exchange(part, "region", nreg, bits[:1]))
    for j in range(1, len(bits), 2):
        part = join(exchange(part, "region", nreg, bits[j : j + 2]))
    bits = bits_of(nind)
    for bit in bits[2:]:
        part = join(exchange(part, "industry", nind, [bit]))
    sums = exchange(part, "industry", nind, bits[:2])
    cell, row_y, col_y = pl.pallas_call(
        functools.partial(finish_kernel, rows, sizes, inds, probs, nind, iters, len(sums)),
        out_shape=[
            jax.ShapeDtypeStruct(whole, jnp.bfloat16),
            shape(LANES, rows),
            shape(LANES, inds),
        ],
        in_specs=[SMEM_SPEC, ANY_SPEC, ANY_SPEC, VMEM_SPEC if RATIO_IN_VMEM else ANY_SPEC]
        + [VMEM_SPEC] * (2 + len(sums) + 6 * iters),
        out_specs=[ANY_SPEC, VMEM_SPEC, VMEM_SPEC],
        scratch_shapes=[
            pltpu.VMEM((rows, LANES), F32),
            pltpu.VMEM((LANES, inds), F32),
            pltpu.VMEM((BLOCK, sizes, inds), F32),
            pltpu.VMEM((LANES, BLOCK), F32),
        ],
        compiler_params=params(),
        name="finish",
    )(info, position, upper_bound, ratio, drow, dcol, *sums, *row_p, *col_p)
    row_step = row_y.reshape(probs, sizes, rows).transpose(0, 2, 1)
    col_step = col_y.reshape(probs, sizes, inds)
    return cell, row_step, col_step


def solution(mesh):
    nreg, nind = mesh.shape["region"], mesh.shape["industry"]
    cells = P(None, "region", None, "industry")
    table = P("region", None, "industry")
    row, col = P(None, "region", None), P(None, None, "industry")
    return jax.shard_map(
        functools.partial(local, nreg, nind, 3),
        mesh=mesh,
        in_specs=(cells, cells, cells, table, table, P(), P(), row, col),
        out_specs=(cells, row, col),
        check_vma=False,
    )
```

```python
import functools

import jax
import jax.numpy as jnp
from jax import lax
from jax.experimental import pallas as pl
from jax.experimental.pallas import tpu as pltpu
from jax.sharding import PartitionSpec as P

WEIGHT_ATTACK = 8.0
SHIFT_DIAG = 1.0
BLOCK = 8
LANES = 128
VMEM_MIB = 12
VMEM_SPEC = pl.BlockSpec(memory_space=pltpu.VMEM)
SMEM_SPEC = pl.BlockSpec(memory_space=pltpu.SMEM)
ANY_SPEC = pl.BlockSpec(memory_space=pl.ANY)
F32 = jnp.float32


def shape(*dims):
    return jax.ShapeDtypeStruct(dims, F32)


def params():
    return pltpu.CompilerParams(vmem_limit_bytes=VMEM_MIB * 1024 * 1024)


def inverse(x):
    rough = pl.reciprocal(x, approx=True)
    return rough * (2.0 - x * rough)


def widen(rows):
    return jnp.broadcast_to(rows[:, None, :], (BLOCK, 8, LANES))


def turned(x):
    return lax.dot_general(
        identity(x.shape[1]), x, (((1,), (1,)), ((), ())), preferred_element_type=F32
    )


def identity(size):
    row = lax.broadcasted_iota(jnp.int32, (size, size), 0)
    return (row == lax.broadcasted_iota(jnp.int32, (size, size), 1)).astype(jnp.bfloat16)


def any_attack(info_ref, first_row):
    hits = jnp.int32(0)
    for k in range(info_ref.shape[0] - 2):
        offset = info_ref[2 + k] - first_row
        hits = hits + jnp.where((offset >= 0) & (offset < BLOCK), 1, 0)
    return hits


def split_halves(full, keep_ref, send_ref, core):
    half = full.shape[-2] // 2
    for ref, which in ((keep_ref, core), (send_ref, 1 - core)):
        ref[...] = full[..., pl.ds(pl.multiple_of(which * half, 8), half), :]


def prepare_kernel(
    rows, sizes, inds, probs, nind,
    info_ref, attack_ref, pos_hbm, low_hbm, high_hbm, upper_hbm, supp_hbm, drow_ref, dcol_ref,
    scaling_ref, barrier_hbm, row_ref, keep_ref, send_ref,
    first_s, second_s, drow_t, dcol_t, col_ref,
):
    blocks = rows // BLOCK
    first_row = info_ref[0] * rows
    first_ind = info_ref[1] * inds
    col_ref[...] = jnp.zeros_like(col_ref)
    drow_t[...] = drow_ref[...].T
    dcol_t[...] = dcol_ref[...].T

    def body(pos_ref, low_ref, high_ref, upper_ref, supp_ref, barrier_ref):
        r0 = pl.multiple_of(pl.program_id(0) * BLOCK, BLOCK)

        def bring(pair, slot):
            for j, ref in enumerate((pos_ref, low_ref, high_ref)):
                both = [ref[:, 2 * pair + r].reshape(LANES, inds) for r in range(2)]
                slot[j] = turned(jnp.concatenate(both, axis=0))
            for j, ref in enumerate((upper_ref, supp_ref)):
                both = []
                for r in range(2):
                    one = ref[2 * pair + r].astype(F32).astype(jnp.bfloat16)
                    both += [one] * probs
                slot[3 + j] = turned(jnp.concatenate(both, axis=0))

        def work(pair, slot, attacked):
            rhs_acc = [jnp.zeros((8, LANES), F32)] * 2
            sum_acc = [jnp.zeros((8, LANES), F32)] * 2
            drow = [
                jnp.broadcast_to(drow_t[pl.ds(r0 + 2 * pair + r, 1), :], (8, LANES)) for r in range(2)
            ]
            for i0 in range(0, inds, 8):
                here = slice(i0, i0 + 8)
                dcol = dcol_t[here, :]
                col_rhs = col_sum_part = None
                for r in range(2):
                    lanes = slice(r * LANES, (r + 1) * LANES)
                    upper = slot[3, here, lanes]
                    active = slot[4, here, lanes]
                    if attacked:
                        lane = lax.broadcasted_iota(jnp.int32, (8, LANES), 1)
                        column = lax.rem(lane, sizes) * (inds * nind) + first_ind + i0
                        column = column + lax.broadcasted_iota(jnp.int32, (8, LANES), 0)
                        row = first_row + r0 + 2 * pair + r
                        hit = (attack_ref[1:2, :] == column) & (attack_ref[0:1, :] == row)
                        active = jnp.where(hit, jnp.ones_like(active), active)
                    value = slot[0, here, lanes] * upper
                    slack = upper - value
                    den = slot[1, here, lanes] * slack + slot[2, here, lanes] * value
                    ratio = active * inverse(den)
                    scaling = value * slack * ratio
                    middle = 0.5 * upper - value
                    barrier = middle * ratio
                    if attacked:
                        barrier = barrier + jnp.where(hit, WEIGHT_ATTACK * scaling, jnp.zeros_like(scaling))
                    margin = middle * active + barrier - scaling * (drow[r] + dcol)
                    scaling_ref[r0 + 2 * pair + r, here, :] = scaling
                    barrier_ref[2 * pair + r, here, :] = barrier
                    rhs_acc[r] = rhs_acc[r] + margin
                    sum_acc[r] = sum_acc[r] + scaling
                    col_rhs = margin if r == 0 else col_rhs + margin
                    col_sum_part = scaling if r == 0 else col_sum_part + scaling
                col_ref[0, here, :] += col_rhs
                col_ref[1, here, :] += col_sum_part
            for r in range(2):
                place = pl.ds(r0 + 2 * pair + r, 1)
                row_ref[0, place, :] = jnp.sum(rhs_acc[r], axis=0, keepdims=True)
                row_ref[1, place, :] = jnp.sum(sum_acc[r], axis=0, keepdims=True)

        hits = any_attack(info_ref, first_row + r0)
        pairs = BLOCK // 2

        @pl.when(hits == 0)
        def _():
            slots = (first_s, second_s)
            bring(0, slots[0])
            for pair in range(pairs):
                if pair + 1 < pairs:
                    bring(pair + 1, slots[(pair + 1) % 2])
                work(pair, slots[pair % 2], False)

        @pl.when(hits != 0)
        def _():
            def step(pair, _):
                bring(pair, first_s)
                work(pair, first_s, True)
                return 0

            lax.fori_loop(0, pairs, step, 0)

    cells = pl.BlockSpec((probs, BLOCK, sizes, inds), lambda b: (0, b, 0, 0))
    shared = pl.BlockSpec((BLOCK, sizes, inds), lambda b: (b, 0, 0))
    turned_cells = pl.BlockSpec((BLOCK, inds, LANES), lambda b: (b, 0, 0))
    pltpu.emit_pipeline(
        body,
        grid=(blocks,),
        in_specs=[cells, cells, cells, shared, shared],
        out_specs=[turned_cells],
    )(pos_hbm, low_hbm, high_hbm, upper_hbm, supp_hbm, barrier_hbm)
    split_halves(col_ref, keep_ref, send_ref, lax.rem(info_ref[0], 2))


def add_up(refs):
    values = [ref[...] for ref in refs]
    while len(values) > 1:
        values = [values[j] + values[j + 1] for j in range(0, len(values), 2)]
    return values[0]


def join_kernel(*refs):
    refs[-1][...] = add_up(refs[:-1])


def begin_kernel(count, info_ref, *refs):
    own, other, row_diag, col_diag, row_now, col_now = refs[count:]
    both = add_up(refs[:count])
    row_diag[...] = both[1] + SHIFT_DIAG
    row_now[...] = both[0] / row_diag[...]
    half = own.shape[1]
    core = lax.rem(info_ref[0], 2)
    for ref, which in ((own, core), (other, 1 - core)):
        here = pl.ds(pl.multiple_of(which * half, 8), half)
        width = ref[1] + SHIFT_DIAG
        col_diag[here, :] = width
        col_now[here, :] = ref[0] / width


def row_end_kernel(*refs):
    refs[-1][...] = add_up(refs[:-2]) / refs[-2][...]


def join_halves(info_ref, own, other, diag, out):
    half = own.shape[0]
    core = lax.rem(info_ref[0], 2)
    for ref, which in ((own, core), (other, 1 - core)):
        here = pl.ds(pl.multiple_of(which * half, 8), half)
        out[here, :] = ref[...] / diag[here, :]


def row_kernel(scaling_ref, col_ref, out_ref):
    rows, inds, _ = scaling_ref.shape

    def step(block, _):
        here = pl.ds(pl.multiple_of(block * BLOCK, BLOCK), BLOCK)
        acc = jnp.zeros((BLOCK, 8, LANES), F32)
        for i0 in range(0, inds, 8):
            acc = acc + scaling_ref[here, i0 : i0 + 8, :] * col_ref[i0 : i0 + 8, :][None]
        out_ref[here, :] = jnp.sum(acc, axis=1)
        return 0

    lax.fori_loop(0, rows // BLOCK, step, 0)


def col_kernel(info_ref, scaling_ref, row_ref, _, keep_ref, send_ref, out_ref):
    rows, inds, _ = scaling_ref.shape
    out_ref[...] = jnp.zeros_like(out_ref)

    def step(block, _):
        here = pl.ds(pl.multiple_of(block * BLOCK, BLOCK), BLOCK)
        row_wide = widen(row_ref[here, :])
        for i0 in range(0, inds, 8):
            out_ref[i0 : i0 + 8, :] += jnp.sum(scaling_ref[here, i0 : i0 + 8, :] * row_wide, axis=0)
        return 0

    lax.fori_loop(0, rows // BLOCK, step, 0)
    split_halves(out_ref, keep_ref, send_ref, lax.rem(info_ref[0], 2))


def products_kernel(iters, nreg, nind, scaling_ref, row_diag_ref, col_diag_ref, *rest):
    count = 3 * iters
    row_p, col_p = [ref[...] for ref in rest[:count]], [ref[...] for ref in rest[count : 2 * count]]
    out_ref, row_z, col_z = rest[2 * count :]
    rows, inds, _ = scaling_ref.shape
    row_zs = [row_p[3 * j] - row_p[3 * j + 1] + row_p[3 * j + 2] for j in range(iters)]
    col_zs = [col_p[3 * j] - col_p[3 * j + 1] + col_p[3 * j + 2] for j in range(iters)]
    row_z[...] = row_zs[-1]
    col_z[...] = col_zs[-1]

    def step(block, acc):
        here = pl.ds(pl.multiple_of(block * BLOCK, BLOCK), BLOCK)
        part = jnp.zeros((BLOCK, 8, LANES), F32)
        for i0 in range(0, inds, 8):
            part = part + scaling_ref[here, i0 : i0 + 8, :] * col_z[i0 : i0 + 8, :][None]
        return acc + jnp.sum(part, axis=1) * row_z[here, :]

    cross = lax.fori_loop(0, rows // BLOCK, step, jnp.zeros((BLOCK, LANES), F32))
    cross = 2.0 * jnp.sum(cross, axis=0, keepdims=True)
    row_diag, col_diag = row_diag_ref[...], col_diag_ref[...]

    def dot(j, row_v, col_v):
        row_sum = jnp.sum(row_zs[j] * row_v, axis=0, keepdims=True)
        col_sum = jnp.sum(col_zs[j] * col_v, axis=0, keepdims=True)
        return row_sum * (1.0 / nind) + col_sum * (1.0 / nreg)

    out_ref[...] = jnp.zeros_like(out_ref)
    slot = 0
    row_n, col_n = row_diag * row_p[0], col_diag * col_p[0]
    for j in range(iters):
        out_ref[slot : slot + 1, :] = dot(j, row_n, col_n)
        slot += 1
    for m in range(iters):
        last = m + 1 == iters
        row_n = row_diag * (row_zs[m] if last else row_p[3 * m] + row_p[3 * m + 3])
        col_n = col_diag * (col_zs[m] if last else col_p[3 * m] + col_p[3 * m + 3])
        for j in range(m, iters):
            product = dot(j, row_n, col_n)
            out_ref[slot : slot + 1, :] = product + cross if last else product
            slot += 1


def finish_kernel(rows, sizes, inds, probs, iters, nsum, scaling_ref, barrier_hbm, drow_ref, dcol_ref, *rest):
    count = 3 * iters
    sums, rest = rest[:nsum], rest[nsum:]
    row_p, col_p = rest[:count], rest[count : 2 * count]
    cell_hbm, row_ref, col_ref, row_add, col_add = rest[2 * count :]
    lane = lax.broadcasted_iota(jnp.int32, (LANES, LANES), 0) // sizes
    other = lax.broadcasted_iota(jnp.int32, (LANES, LANES), 1) // sizes
    same = (lane == other).astype(F32)
    total = jnp.dot(add_up(sums), same, preferred_element_type=F32, precision=lax.Precision.HIGHEST)
    g0, g1, g2, h00, h10, h20, h11, h21, h22 = [total[j : j + 1, :] for j in range(9)]
    l1, l2 = h10 / h00, h20 / h00
    d1 = h11 - l1 * h10
    t21 = h21 - l2 * h10
    m21 = t21 / d1
    d2 = h22 - l2 * h20 - m21 * t21
    y1 = g1 - l1 * g0
    y2 = g2 - l2 * g0 - m21 * y1
    c2 = y2 / d2
    c1 = y1 / d1 - m21 * c2
    c0 = g0 / h00 - l1 * c1 - l2 * c2

    def combine(refs):
        acc = None
        for j, coef in enumerate((c0, c1, c2)):
            term = coef * (refs[3 * j][...] - refs[3 * j + 1][...] + refs[3 * j + 2][...])
            acc = term if acc is None else acc + term
        return acc

    row_y = combine(row_p)
    col_y = combine(col_p)
    row_ref[...] = row_y.T
    col_ref[...] = col_y.T
    row_add[...] = row_y + drow_ref[...].T
    col_add[...] = col_y + dcol_ref[...].T

    def body(barrier_ref, cell_ref):
        r0 = pl.program_id(0) * BLOCK
        for r in range(BLOCK):
            cell = (col_add[...] + row_add[pl.ds(r0 + r, 1), :]) * scaling_ref[r0 + r] - barrier_ref[r]
            cell = turned(cell.astype(jnp.bfloat16))
            cell_ref[:, r] = cell.astype(jnp.bfloat16).reshape(probs, sizes, inds)

    cells = pl.BlockSpec((probs, BLOCK, sizes, inds), lambda b: (0, b, 0, 0))
    turned_cells = pl.BlockSpec((BLOCK, inds, LANES), lambda b: (b, 0, 0))
    pltpu.emit_pipeline(body, grid=(rows // BLOCK,), in_specs=[turned_cells], out_specs=[cells])(
        barrier_hbm, cell_hbm
    )


def bits_of(count):
    return [1 << j for j in range(count.bit_length() - 1)]


def exchange(x, axis, count, bits):
    flips = [0]
    for bit in bits:
        flips = flips + [flip | bit for flip in flips]
    return [x] + [lax.ppermute(x, axis, [(j, j ^ flip) for j in range(count)]) for flip in flips[1:]]


def vmem_call(kernel, outs, name, scratch=(), cost=None, scalars=0):
    def call(*args):
        return pl.pallas_call(
            kernel,
            out_shape=outs,
            in_specs=[SMEM_SPEC] * scalars + [VMEM_SPEC] * (len(args) - scalars),
            out_specs=[VMEM_SPEC] * len(outs),
            scratch_shapes=list(scratch),
            compiler_params=params(),
            cost_estimate=cost,
            name=name,
        )(*args)

    return call


def join(parts):
    return vmem_call(join_kernel, [shape(*parts[0].shape)], "join")(*parts)[0]


def row_sum(x, nind):
    parts = [x]
    for bit in bits_of(nind):
        if len(parts) > 1:
            x = join(parts)
        parts = exchange(x, "industry", nind, [bit])
    return parts


def col_sum(keep, send, nreg):
    (arrived,) = exchange(send, "region", nreg, [1])[1:]
    x = join([keep, arrived])
    bits = bits_of(nreg)[1:]
    for j in range(0, len(bits), 2):
        x = join(exchange(x, "region", nreg, bits[j : j + 2]))
    return exchange(x, "region", nreg, [1])


def local(
    nreg, nind, iters,
    position, dual_lower, dual_upper, upper_bound, suppressed,
    attack_region, attack_column, dual_row, dual_col,
):
    probs, rows, sizes, inds = position.shape
    my_reg, my_ind = lax.axis_index("region"), lax.axis_index("industry")
    info = jnp.concatenate([jnp.stack([my_reg, my_ind]).astype(jnp.int32), attack_region])
    attack = jnp.repeat(jnp.stack([attack_region, attack_column]), sizes, axis=1)
    drow = dual_row.transpose(0, 2, 1).reshape(LANES, rows)
    dcol = dual_col.reshape(LANES, inds)
    half = inds // 2

    def in_hbm(x):
        return pltpu.with_memory_space_constraint(x, pltpu.HBM)

    def keep(x):
        return pltpu.with_memory_space_constraint(x, pltpu.VMEM)

    position, dual_lower, dual_upper = map(in_hbm, (position, dual_lower, dual_upper))
    upper_bound, suppressed = map(in_hbm, (upper_bound, suppressed))
    scaling, barrier, row_both, col_keep, col_send = pl.pallas_call(
        functools.partial(prepare_kernel, rows, sizes, inds, probs, nind),
        out_shape=[
            pltpu.VMEM((rows, inds, LANES), F32),
            shape(rows, inds, LANES),
            shape(2, rows, LANES),
            shape(2, half, LANES),
            shape(2, half, LANES),
        ],
        in_specs=[SMEM_SPEC, VMEM_SPEC] + [ANY_SPEC] * 5 + [VMEM_SPEC] * 2,
        out_specs=[VMEM_SPEC, ANY_SPEC] + [VMEM_SPEC] * 3,
        scratch_shapes=[
            pltpu.VMEM((5, inds, 2 * LANES), F32),
            pltpu.VMEM((5, inds, 2 * LANES), F32),
            pltpu.VMEM((rows, LANES), F32),
            pltpu.VMEM((inds, LANES), F32),
            pltpu.VMEM((2, inds, LANES), F32),
        ],
        compiler_params=params(),
        name="prepare",
    )(info, attack, position, dual_lower, dual_upper, upper_bound, suppressed, drow, dcol)
    scaling = keep(scaling)
    barrier = in_hbm(barrier)
    cells = rows * inds * LANES
    cost = pl.CostEstimate(flops=2 * cells, bytes_accessed=4 * cells, transcendentals=0)
    margins = [shape(rows, LANES), shape(inds, LANES)]
    row_parts = row_sum(row_both, nind)
    col_halves = col_sum(col_keep, col_send, nreg)
    kernel = functools.partial(begin_kernel, len(row_parts))
    row_diag, col_diag, row_now, col_now = vmem_call(kernel, margins * 2, "begin", scalars=1)(
        info, *row_parts, *col_halves
    )
    row_p, col_p = [row_now], [col_now]
    for _ in range(3 * iters - 1):
        (row_out,) = vmem_call(row_kernel, margins[:1], "row_sweep", cost=cost)(scaling, col_p[-1])
        col_keep, col_send = vmem_call(
            col_kernel, [shape(half, LANES)] * 2, "col_sweep", [pltpu.VMEM((inds, LANES), F32)], cost, 1
        )(info, scaling, row_p[-1], row_out)
        row_parts = row_sum(row_out, nind)
        col_halves = col_sum(col_keep, col_send, nreg)
        row_p += vmem_call(row_end_kernel, margins[:1], "row_end")(*row_parts, row_diag)
        col_p += vmem_call(join_halves, margins[1:], "col_end", scalars=1)(info, *col_halves, col_diag)
    kernel = functools.partial(products_kernel, iters, nreg, nind)
    scratch = [pltpu.VMEM((rows, LANES), F32), pltpu.VMEM((inds, LANES), F32)]
    (part,) = vmem_call(kernel, [shape(16, LANES)], "products", scratch)(
        scaling, row_diag, col_diag, *row_p, *col_p
    )
    bits = bits_of(nreg)
    part = join(exchange(part, "region", nreg, bits[:1]))
    for j in range(1, len(bits), 2):
        part = join(exchange(part, "region", nreg, bits[j : j + 2]))
    bits = bits_of(nind)
    for bit in bits[2:]:
        part = join(exchange(part, "industry", nind, [bit]))
    sums = exchange(part, "industry", nind, bits[:2])
    cell, row_y, col_y = pl.pallas_call(
        functools.partial(finish_kernel, rows, sizes, inds, probs, iters, len(sums)),
        out_shape=[
            jax.ShapeDtypeStruct((probs, rows, sizes, inds), jnp.bfloat16),
            shape(LANES, rows),
            shape(LANES, inds),
        ],
        in_specs=[VMEM_SPEC, ANY_SPEC] + [VMEM_SPEC] * (2 + len(sums) + 6 * iters),
        out_specs=[ANY_SPEC, VMEM_SPEC, VMEM_SPEC],
        scratch_shapes=[pltpu.VMEM((rows, LANES), F32), pltpu.VMEM((inds, LANES), F32)],
        compiler_params=params(),
        name="finish",
    )(scaling, barrier, drow, dcol, *sums, *row_p, *col_p)
    row_step = row_y.reshape(probs, sizes, rows).transpose(0, 2, 1)
    col_step = col_y.reshape(probs, sizes, inds)
    return cell, row_step, col_step


def solution(mesh):
    nreg, nind = mesh.shape["region"], mesh.shape["industry"]
    cells = P(None, "region", None, "industry")
    table = P("region", None, "industry")
    row, col = P(None, "region", None), P(None, None, "industry")
    return jax.shard_map(
        functools.partial(local, nreg, nind, 3),
        mesh=mesh,
        in_specs=(cells, cells, cells, table, table, P(), P(), row, col),
        out_specs=(cells, row, col),
        check_vma=False,
    )
```

```python
import functools

import jax
import jax.numpy as jnp
from jax import lax
from jax.experimental import pallas as pl
from jax.experimental.pallas import tpu as pltpu
from jax.sharding import PartitionSpec as P

WEIGHT_ATTACK = 8.0
SHIFT_DIAG = 1.0
BLOCK = 8
LANES = 128
VMEM_MIB = 12
VMEM_SPEC = pl.BlockSpec(memory_space=pltpu.VMEM)
SMEM_SPEC = pl.BlockSpec(memory_space=pltpu.SMEM)
ANY_SPEC = pl.BlockSpec(memory_space=pl.ANY)
F32 = jnp.float32


def shape(*dims):
    return jax.ShapeDtypeStruct(dims, F32)


def params():
    return pltpu.CompilerParams(vmem_limit_bytes=VMEM_MIB * 1024 * 1024)


def inverse(x):
    rough = pl.reciprocal(x, approx=True)
    return rough * (2.0 - x * rough)


def widen(rows):
    return jnp.broadcast_to(rows[:, None, :], (BLOCK, 8, LANES))


def turned(x):
    return lax.dot_general(
        identity(x.shape[1]), x, (((1,), (1,)), ((), ())), preferred_element_type=F32
    )


def identity(size):
    row = lax.broadcasted_iota(jnp.int32, (size, size), 0)
    return (row == lax.broadcasted_iota(jnp.int32, (size, size), 1)).astype(jnp.bfloat16)


def any_attack(info_ref, first_row):
    hits = jnp.int32(0)
    for k in range((info_ref.shape[0] - 2) // 2):
        offset = info_ref[2 + k] - first_row
        hits = hits + jnp.where((offset >= 0) & (offset < BLOCK), 1, 0)
    return hits


def split_halves(full, keep_ref, send_ref, odd_ref):
    half = full.shape[-2] // 2
    odd = jnp.broadcast_to(odd_ref[0:1, :] > 0, keep_ref.shape)
    first, second = full[..., :half, :], full[..., half:, :]
    keep_ref[...] = jnp.where(odd, second, first)
    send_ref[...] = jnp.where(odd, first, second)


def prepare_kernel(
    rows, sizes, inds, probs, nind,
    info_ref, odd_ref, pos_hbm, low_hbm, high_hbm, upper_hbm, supp_hbm, drow_ref, dcol_ref,
    scaling_ref, barrier_hbm, row_ref, keep_ref, send_ref,
    first_s, second_s, drow_t, dcol_t, col_ref,
):
    blocks = rows // BLOCK
    first_row = info_ref[0] * rows
    first_ind = info_ref[1] * inds
    col_ref[...] = jnp.zeros_like(col_ref)
    drow_t[...] = drow_ref[...].T
    dcol_t[...] = dcol_ref[...].T

    def body(pos_ref, low_ref, high_ref, upper_ref, supp_ref, barrier_ref):
        r0 = pl.multiple_of(pl.program_id(0) * BLOCK, BLOCK)

        def bring(pair, slot):
            for j, ref in enumerate((pos_ref, low_ref, high_ref)):
                both = [ref[:, 2 * pair + r].reshape(LANES, inds) for r in range(2)]
                slot[j] = turned(jnp.concatenate(both, axis=0))
            for j, ref in enumerate((upper_ref, supp_ref)):
                both = []
                for r in range(2):
                    one = ref[2 * pair + r].astype(F32).astype(jnp.bfloat16)
                    both += [one] * probs
                slot[3 + j] = turned(jnp.concatenate(both, axis=0))

        def work(pair, slot, attacked):
            rhs_acc = [jnp.zeros((8, LANES), F32)] * 2
            sum_acc = [jnp.zeros((8, LANES), F32)] * 2
            drow = [
                jnp.broadcast_to(drow_t[pl.ds(r0 + 2 * pair + r, 1), :], (8, LANES)) for r in range(2)
            ]
            for i0 in range(0, inds, 8):
                here = slice(i0, i0 + 8)
                dcol = dcol_t[here, :]
                col_rhs = col_sum_part = None
                for r in range(2):
                    lanes = slice(r * LANES, (r + 1) * LANES)
                    upper = slot[3, here, lanes]
                    active = slot[4, here, lanes]
                    if attacked:
                        lane = lax.broadcasted_iota(jnp.int32, (8, LANES), 1)
                        column = lax.rem(lane, sizes) * (inds * nind) + first_ind + i0
                        column = column + lax.broadcasted_iota(jnp.int32, (8, LANES), 0)
                        row = first_row + r0 + 2 * pair + r
                        goal = jnp.full((8, LANES), -1, jnp.int32)
                        for k in range(probs):
                            mine = jnp.where(info_ref[2 + k] == row, info_ref[2 + probs + k], -1)
                            goal = jnp.where(lane // sizes == k, mine, goal)
                        hit = goal == column
                        active = jnp.where(hit, jnp.ones_like(active), active)
                    value = slot[0, here, lanes] * upper
                    slack = upper - value
                    den = slot[1, here, lanes] * slack + slot[2, here, lanes] * value
                    ratio = active * inverse(den)
                    scaling = value * slack * ratio
                    middle = 0.5 * upper - value
                    barrier = middle * ratio
                    if attacked:
                        barrier = barrier + jnp.where(hit, WEIGHT_ATTACK * scaling, jnp.zeros_like(scaling))
                    margin = middle * active + barrier - scaling * (drow[r] + dcol)
                    scaling_ref[r0 + 2 * pair + r, here, :] = scaling
                    barrier_ref[2 * pair + r, here, :] = barrier
                    rhs_acc[r] = rhs_acc[r] + margin
                    sum_acc[r] = sum_acc[r] + scaling
                    col_rhs = margin if r == 0 else col_rhs + margin
                    col_sum_part = scaling if r == 0 else col_sum_part + scaling
                col_ref[0, here, :] += col_rhs
                col_ref[1, here, :] += col_sum_part
            for r in range(2):
                place = pl.ds(r0 + 2 * pair + r, 1)
                row_ref[0, place, :] = jnp.sum(rhs_acc[r], axis=0, keepdims=True)
                row_ref[1, place, :] = jnp.sum(sum_acc[r], axis=0, keepdims=True)

        hits = any_attack(info_ref, first_row + r0)
        pairs = BLOCK // 2

        @pl.when(hits == 0)
        def _():
            slots = (first_s, second_s)
            bring(0, slots[0])
            for pair in range(pairs):
                if pair + 1 < pairs:
                    bring(pair + 1, slots[(pair + 1) % 2])
                work(pair, slots[pair % 2], False)

        @pl.when(hits != 0)
        def _():
            def step(pair, _):
                bring(pair, first_s)
                work(pair, first_s, True)
                return 0

            lax.fori_loop(0, pairs, step, 0)

    deep = pl.Buffered(3)
    cells = pl.BlockSpec((probs, BLOCK, sizes, inds), lambda b: (0, b, 0, 0), pipeline_mode=deep)
    shared = pl.BlockSpec((BLOCK, sizes, inds), lambda b: (b, 0, 0), pipeline_mode=deep)
    turned_cells = pl.BlockSpec((BLOCK, inds, LANES), lambda b: (b, 0, 0))
    pltpu.emit_pipeline(
        body,
        grid=(blocks,),
        in_specs=[cells, cells, cells, shared, shared],
        out_specs=[turned_cells],
    )(pos_hbm, low_hbm, high_hbm, upper_hbm, supp_hbm, barrier_hbm)
    split_halves(col_ref, keep_ref, send_ref, odd_ref)


def add_up(refs):
    values = [ref[...] for ref in refs]
    while len(values) > 1:
        values = [values[j] + values[j + 1] for j in range(0, len(values), 2)]
    return values[0]


def join_kernel(*refs):
    refs[-1][...] = add_up(refs[:-1])


def begin_kernel(count, odd_ref, *refs):
    own, other, row_diag, col_diag, row_now, col_now = refs[count:]
    both = add_up(refs[:count])
    row_diag[...] = both[1] + SHIFT_DIAG
    row_now[...] = both[0] / row_diag[...]
    half = own.shape[1]
    odd = jnp.broadcast_to(odd_ref[0:1, :] > 0, own.shape)
    halves = jnp.where(odd, other[...], own[...]), jnp.where(odd, own[...], other[...])
    for j, part in enumerate(halves):
        here = slice(j * half, (j + 1) * half)
        width = part[1] + SHIFT_DIAG
        col_diag[here, :] = width
        col_now[here, :] = part[0] / width


def row_end_kernel(*refs):
    refs[-1][...] = add_up(refs[:-2]) / refs[-2][...]


def join_halves(odd_ref, own, other, diag, out):
    half = own.shape[0]
    odd = jnp.broadcast_to(odd_ref[0:1, :] > 0, own.shape)
    out[:half, :] = jnp.where(odd, other[...], own[...]) / diag[:half, :]
    out[half:, :] = jnp.where(odd, own[...], other[...]) / diag[half:, :]


def row_kernel(scaling_ref, col_ref, out_ref):
    rows, inds, _ = scaling_ref.shape

    def step(block, _):
        here = pl.ds(pl.multiple_of(block * BLOCK, BLOCK), BLOCK)
        acc = jnp.zeros((BLOCK, 8, LANES), F32)
        for i0 in range(0, inds, 8):
            acc = acc + scaling_ref[here, i0 : i0 + 8, :] * col_ref[i0 : i0 + 8, :][None]
        out_ref[here, :] = jnp.sum(acc, axis=1)
        return 0

    lax.fori_loop(0, rows // BLOCK, step, 0)


def col_kernel(odd_ref, scaling_ref, row_ref, _, keep_ref, send_ref, out_ref):
    rows, inds, _ = scaling_ref.shape
    out_ref[...] = jnp.zeros_like(out_ref)

    def step(block, _):
        here = pl.ds(pl.multiple_of(block * BLOCK, BLOCK), BLOCK)
        row_wide = widen(row_ref[here, :])
        for i0 in range(0, inds, 8):
            out_ref[i0 : i0 + 8, :] += jnp.sum(scaling_ref[here, i0 : i0 + 8, :] * row_wide, axis=0)
        return 0

    lax.fori_loop(0, rows // BLOCK, step, 0)
    split_halves(out_ref, keep_ref, send_ref, odd_ref)


def products_kernel(iters, nreg, nind, scaling_ref, row_diag_ref, col_diag_ref, *rest):
    count = 3 * iters
    row_p, col_p = [ref[...] for ref in rest[:count]], [ref[...] for ref in rest[count : 2 * count]]
    out_ref, row_z, col_z = rest[2 * count :]
    rows, inds, _ = scaling_ref.shape
    row_zs = [row_p[3 * j] - row_p[3 * j + 1] + row_p[3 * j + 2] for j in range(iters)]
    col_zs = [col_p[3 * j] - col_p[3 * j + 1] + col_p[3 * j + 2] for j in range(iters)]
    row_z[...] = row_zs[-1]
    col_z[...] = col_zs[-1]

    def step(block, acc):
        here = pl.ds(pl.multiple_of(block * BLOCK, BLOCK), BLOCK)
        part = jnp.zeros((BLOCK, 8, LANES), F32)
        for i0 in range(0, inds, 8):
            part = part + scaling_ref[here, i0 : i0 + 8, :] * col_z[i0 : i0 + 8, :][None]
        return acc + jnp.sum(part, axis=1) * row_z[here, :]

    cross = lax.fori_loop(0, rows // BLOCK, step, jnp.zeros((BLOCK, LANES), F32))
    cross = 2.0 * jnp.sum(cross, axis=0, keepdims=True)
    row_diag, col_diag = row_diag_ref[...], col_diag_ref[...]

    def dot(j, row_v, col_v):
        row_sum = jnp.sum(row_zs[j] * row_v, axis=0, keepdims=True)
        col_sum = jnp.sum(col_zs[j] * col_v, axis=0, keepdims=True)
        return row_sum * (1.0 / nind) + col_sum * (1.0 / nreg)

    out_ref[...] = jnp.zeros_like(out_ref)
    slot = 0
    row_n, col_n = row_diag * row_p[0], col_diag * col_p[0]
    for j in range(iters):
        out_ref[slot : slot + 1, :] = dot(j, row_n, col_n)
        slot += 1
    for m in range(iters):
        last = m + 1 == iters
        row_n = row_diag * (row_zs[m] if last else row_p[3 * m] + row_p[3 * m + 3])
        col_n = col_diag * (col_zs[m] if last else col_p[3 * m] + col_p[3 * m + 3])
        for j in range(m, iters):
            product = dot(j, row_n, col_n)
            out_ref[slot : slot + 1, :] = product + cross if last else product
            slot += 1


def finish_kernel(rows, sizes, inds, probs, iters, nsum, scaling_ref, barrier_hbm, drow_ref, dcol_ref, *rest):
    count = 3 * iters
    sums, rest = rest[:nsum], rest[nsum:]
    row_p, col_p = rest[:count], rest[count : 2 * count]
    cell_hbm, row_ref, col_ref, row_add, col_add = rest[2 * count :]
    lane = lax.broadcasted_iota(jnp.int32, (LANES, LANES), 0) // sizes
    other = lax.broadcasted_iota(jnp.int32, (LANES, LANES), 1) // sizes
    same = (lane == other).astype(F32)
    total = jnp.dot(add_up(sums), same, preferred_element_type=F32, precision=lax.Precision.HIGHEST)
    g0, g1, g2, h00, h10, h20, h11, h21, h22 = [total[j : j + 1, :] for j in range(9)]
    l1, l2 = h10 / h00, h20 / h00
    d1 = h11 - l1 * h10
    t21 = h21 - l2 * h10
    m21 = t21 / d1
    d2 = h22 - l2 * h20 - m21 * t21
    y1 = g1 - l1 * g0
    y2 = g2 - l2 * g0 - m21 * y1
    c2 = y2 / d2
    c1 = y1 / d1 - m21 * c2
    c0 = g0 / h00 - l1 * c1 - l2 * c2

    def combine(refs):
        acc = None
        for j, coef in enumerate((c0, c1, c2)):
            term = coef * (refs[3 * j][...] - refs[3 * j + 1][...] + refs[3 * j + 2][...])
            acc = term if acc is None else acc + term
        return acc

    row_y = combine(row_p)
    col_y = combine(col_p)
    row_ref[...] = row_y.T
    col_ref[...] = col_y.T
    row_add[...] = row_y + drow_ref[...].T
    col_add[...] = col_y + dcol_ref[...].T

    def body(barrier_ref, cell_ref):
        r0 = pl.program_id(0) * BLOCK
        for r in range(BLOCK):
            cell = (col_add[...] + row_add[pl.ds(r0 + r, 1), :]) * scaling_ref[r0 + r] - barrier_ref[r]
            cell = turned(cell.astype(jnp.bfloat16))
            cell_ref[:, r] = cell.astype(jnp.bfloat16).reshape(probs, sizes, inds)

    deep = pl.Buffered(4)
    cells = pl.BlockSpec((probs, BLOCK, sizes, inds), lambda b: (0, b, 0, 0))
    turned_cells = pl.BlockSpec((BLOCK, inds, LANES), lambda b: (b, 0, 0), pipeline_mode=deep)
    pltpu.emit_pipeline(body, grid=(rows // BLOCK,), in_specs=[turned_cells], out_specs=[cells])(
        barrier_hbm, cell_hbm
    )


def bits_of(count):
    return [1 << j for j in range(count.bit_length() - 1)]


def exchange(x, axis, count, bits):
    flips = [0]
    for bit in bits:
        flips = flips + [flip | bit for flip in flips]
    return [x] + [lax.ppermute(x, axis, [(j, j ^ flip) for j in range(count)]) for flip in flips[1:]]


def vmem_call(kernel, outs, name, scratch=(), cost=None):
    def call(*args):
        return pl.pallas_call(
            kernel,
            out_shape=outs,
            in_specs=[VMEM_SPEC] * len(args),
            out_specs=[VMEM_SPEC] * len(outs),
            scratch_shapes=list(scratch),
            compiler_params=params(),
            cost_estimate=cost,
            name=name,
        )(*args)

    return call


def join(parts):
    return vmem_call(join_kernel, [shape(*parts[0].shape)], "join")(*parts)[0]


def row_sum(x, nind):
    parts = [x]
    for bit in bits_of(nind):
        if len(parts) > 1:
            x = join(parts)
        parts = exchange(x, "industry", nind, [bit])
    return parts


def col_sum(keep, send, nreg):
    (arrived,) = exchange(send, "region", nreg, [1])[1:]
    x = join([keep, arrived])
    bits = bits_of(nreg)[1:]
    for j in range(0, len(bits), 2):
        x = join(exchange(x, "region", nreg, bits[j : j + 2]))
    return exchange(x, "region", nreg, [1])


def local(
    nreg, nind, iters,
    position, dual_lower, dual_upper, upper_bound, suppressed,
    attack_region, attack_column, dual_row, dual_col,
):
    probs, rows, sizes, inds = position.shape
    my_reg, my_ind = lax.axis_index("region"), lax.axis_index("industry")
    info = jnp.concatenate([jnp.stack([my_reg, my_ind]).astype(jnp.int32), attack_region, attack_column])
    odd = jnp.broadcast_to(lax.rem(my_reg, 2).astype(F32), (8, LANES))
    drow = dual_row.transpose(0, 2, 1).reshape(LANES, rows)
    dcol = dual_col.reshape(LANES, inds)
    half = inds // 2

    def in_hbm(x):
        return pltpu.with_memory_space_constraint(x, pltpu.HBM)

    def keep(x):
        return pltpu.with_memory_space_constraint(x, pltpu.VMEM)

    position, dual_lower, dual_upper = map(in_hbm, (position, dual_lower, dual_upper))
    upper_bound, suppressed = map(in_hbm, (upper_bound, suppressed))
    scaling, barrier, row_both, col_keep, col_send = pl.pallas_call(
        functools.partial(prepare_kernel, rows, sizes, inds, probs, nind),
        out_shape=[
            pltpu.VMEM((rows, inds, LANES), F32),
            shape(rows, inds, LANES),
            shape(2, rows, LANES),
            shape(2, half, LANES),
            shape(2, half, LANES),
        ],
        in_specs=[SMEM_SPEC, VMEM_SPEC] + [ANY_SPEC] * 5 + [VMEM_SPEC] * 2,
        out_specs=[VMEM_SPEC, ANY_SPEC] + [VMEM_SPEC] * 3,
        scratch_shapes=[
            pltpu.VMEM((5, inds, 2 * LANES), F32),
            pltpu.VMEM((5, inds, 2 * LANES), F32),
            pltpu.VMEM((rows, LANES), F32),
            pltpu.VMEM((inds, LANES), F32),
            pltpu.VMEM((2, inds, LANES), F32),
        ],
        compiler_params=params(),
        name="prepare",
    )(info, odd, position, dual_lower, dual_upper, upper_bound, suppressed, drow, dcol)
    scaling = keep(scaling)
    barrier = in_hbm(barrier)
    cells = rows * inds * LANES
    cost = pl.CostEstimate(flops=2 * cells, bytes_accessed=4 * cells, transcendentals=0)
    margins = [shape(rows, LANES), shape(inds, LANES)]
    row_parts = row_sum(row_both, nind)
    col_halves = col_sum(col_keep, col_send, nreg)
    kernel = functools.partial(begin_kernel, len(row_parts))
    row_diag, col_diag, row_now, col_now = vmem_call(kernel, margins * 2, "begin")(
        odd, *row_parts, *col_halves
    )
    row_p, col_p = [row_now], [col_now]
    for _ in range(3 * iters - 1):
        (row_out,) = vmem_call(row_kernel, margins[:1], "row_sweep", cost=cost)(scaling, col_p[-1])
        col_keep, col_send = vmem_call(
            col_kernel, [shape(half, LANES)] * 2, "col_sweep", [pltpu.VMEM((inds, LANES), F32)], cost
        )(odd, scaling, row_p[-1], row_out)
        row_parts = row_sum(row_out, nind)
        col_halves = col_sum(col_keep, col_send, nreg)
        row_p += vmem_call(row_end_kernel, margins[:1], "row_end")(*row_parts, row_diag)
        col_p += vmem_call(join_halves, margins[1:], "col_end")(odd, *col_halves, col_diag)
    kernel = functools.partial(products_kernel, iters, nreg, nind)
    scratch = [pltpu.VMEM((rows, LANES), F32), pltpu.VMEM((inds, LANES), F32)]
    (part,) = vmem_call(kernel, [shape(16, LANES)], "products", scratch)(
        scaling, row_diag, col_diag, *row_p, *col_p
    )
    bits = bits_of(nreg)
    part = join(exchange(part, "region", nreg, bits[:1]))
    for j in range(1, len(bits), 2):
        part = join(exchange(part, "region", nreg, bits[j : j + 2]))
    bits = bits_of(nind)
    for bit in bits[2:]:
        part = join(exchange(part, "industry", nind, [bit]))
    sums = exchange(part, "industry", nind, bits[:2])
    cell, row_y, col_y = pl.pallas_call(
        functools.partial(finish_kernel, rows, sizes, inds, probs, iters, len(sums)),
        out_shape=[
            jax.ShapeDtypeStruct((probs, rows, sizes, inds), jnp.bfloat16),
            shape(LANES, rows),
            shape(LANES, inds),
        ],
        in_specs=[VMEM_SPEC, ANY_SPEC] + [VMEM_SPEC] * (2 + len(sums) + 6 * iters),
        out_specs=[ANY_SPEC, VMEM_SPEC, VMEM_SPEC],
        scratch_shapes=[pltpu.VMEM((rows, LANES), F32), pltpu.VMEM((inds, LANES), F32)],
        compiler_params=params(),
        name="finish",
    )(scaling, barrier, drow, dcol, *sums, *row_p, *col_p)
    row_step = row_y.reshape(probs, sizes, rows).transpose(0, 2, 1)
    col_step = col_y.reshape(probs, sizes, inds)
    return cell, row_step, col_step


def solution(mesh):
    nreg, nind = mesh.shape["region"], mesh.shape["industry"]
    cells = P(None, "region", None, "industry")
    table = P("region", None, "industry")
    row, col = P(None, "region", None), P(None, None, "industry")
    return jax.shard_map(
        functools.partial(local, nreg, nind, 3),
        mesh=mesh,
        in_specs=(cells, cells, cells, table, table, P(), P(), row, col),
        out_specs=(cells, row, col),
        check_vma=False,
    )
```

```python
import functools

import jax
import jax.numpy as jnp
from jax import lax
from jax.experimental import pallas as pl
from jax.experimental.pallas import tpu as pltpu
from jax.sharding import PartitionSpec as P

WEIGHT_ATTACK = 8.0
SHIFT_DIAG = 1.0
SUPPRESSED = 64
BLOCK = 8
ARRAYS = 4
LANES = 128
VMEM_MIB = 12
VMEM_SPEC = pl.BlockSpec(memory_space=pltpu.VMEM)
SMEM_SPEC = pl.BlockSpec(memory_space=pltpu.SMEM)
ANY_SPEC = pl.BlockSpec(memory_space=pl.ANY)
F32 = jnp.float32


def shape(*dims):
    return jax.ShapeDtypeStruct(dims, F32)


def params():
    return pltpu.CompilerParams(vmem_limit_bytes=VMEM_MIB * 1024 * 1024)


def inverse(x):
    rough = pl.reciprocal(x, approx=True)
    return rough * (2.0 - x * rough)


def widen(rows):
    return jnp.broadcast_to(rows[:, None, :], (BLOCK, 8, LANES))


def turned(x):
    return lax.dot_general(
        identity(x.shape[1]), x, (((1,), (1,)), ((), ())), preferred_element_type=F32
    )


def identity(size):
    row = lax.broadcasted_iota(jnp.int32, (size, size), 0)
    return (row == lax.broadcasted_iota(jnp.int32, (size, size), 1)).astype(jnp.bfloat16)


def any_attack(info_ref, first_row):
    hits = jnp.int32(0)
    for k in range((info_ref.shape[0] - 2) // 2):
        offset = info_ref[2 + k] - first_row
        hits = hits + jnp.where((offset >= 0) & (offset < BLOCK), 1, 0)
    return hits


def split_halves(full, keep_ref, send_ref, odd_ref):
    half = full.shape[-2] // 2
    odd = jnp.broadcast_to(odd_ref[0:1, :] > 0, keep_ref.shape)
    first, second = full[..., :half, :], full[..., half:, :]
    keep_ref[...] = jnp.where(odd, second, first)
    send_ref[...] = jnp.where(odd, first, second)


def prepare_kernel(
    rows, sizes, inds, probs, nind,
    info_ref, odd_ref, pos_hbm, low_hbm, high_hbm, upper_hbm, supp_hbm, drow_ref, dcol_ref,
    scaling_ref, barrier_hbm, row_ref, keep_ref, send_ref,
    first_s, second_s, drow_t, dcol_t, col_ref,
):
    blocks = rows // BLOCK
    first_row = info_ref[0] * rows
    first_ind = info_ref[1] * inds
    col_ref[...] = jnp.zeros_like(col_ref)
    drow_t[...] = drow_ref[...].T
    dcol_t[...] = dcol_ref[...].T

    def body(pos_ref, low_ref, high_ref, upper_ref, supp_ref, barrier_ref):
        r0 = pl.multiple_of(pl.program_id(0) * BLOCK, BLOCK)

        def bring(pair, slot, j):
            both = []
            for r in range(2):
                if j < 3:
                    both += [(pos_ref, low_ref, high_ref)[j][:, 2 * pair + r].reshape(LANES, inds)]
                else:
                    coded = upper_ref[2 * pair + r] + SUPPRESSED * supp_ref[2 * pair + r]
                    both += [coded.astype(F32).astype(jnp.bfloat16)] * probs
            slot[j] = turned(jnp.concatenate(both, axis=0))

        def work(pair, slot, attacked, next_slot=None):
            rhs_acc = [jnp.zeros((8, LANES), F32)] * 2
            sum_acc = [jnp.zeros((8, LANES), F32)] * 2
            drow = [
                jnp.broadcast_to(drow_t[pl.ds(r0 + 2 * pair + r, 1), :], (8, LANES)) for r in range(2)
            ]
            for i0 in range(0, inds, 8):
                here = slice(i0, i0 + 8)
                if next_slot is not None and i0 * ARRAYS // inds != (i0 - 8) * ARRAYS // inds:
                    bring(pair + 1, next_slot, i0 * ARRAYS // inds)
                dcol = dcol_t[here, :]
                col_rhs = col_sum_part = None
                for r in range(2):
                    lanes = slice(r * LANES, (r + 1) * LANES)
                    coded = slot[3, here, lanes]
                    suppressed = coded >= SUPPRESSED
                    upper = jnp.where(suppressed, coded - SUPPRESSED, coded)
                    active = jnp.where(suppressed, jnp.ones_like(coded), jnp.zeros_like(coded))
                    if attacked:
                        lane = lax.broadcasted_iota(jnp.int32, (8, LANES), 1)
                        column = lax.rem(lane, sizes) * (inds * nind) + first_ind + i0
                        column = column + lax.broadcasted_iota(jnp.int32, (8, LANES), 0)
                        row = first_row + r0 + 2 * pair + r
                        goal = jnp.full((8, LANES), -1, jnp.int32)
                        for k in range(probs):
                            mine = jnp.where(info_ref[2 + k] == row, info_ref[2 + probs + k], -1)
                            goal = jnp.where(lane // sizes == k, mine, goal)
                        hit = goal == column
                        active = jnp.where(hit, jnp.ones_like(active), active)
                    value = slot[0, here, lanes] * upper
                    slack = upper - value
                    den = slot[1, here, lanes] * slack + slot[2, here, lanes] * value
                    ratio = active * inverse(den)
                    scaling = value * slack * ratio
                    middle = 0.5 * upper - value
                    barrier = middle * ratio
                    if attacked:
                        barrier = barrier + jnp.where(hit, WEIGHT_ATTACK * scaling, jnp.zeros_like(scaling))
                    margin = middle * active + barrier - scaling * (drow[r] + dcol)
                    scaling_ref[r0 + 2 * pair + r, here, :] = scaling
                    barrier_ref[2 * pair + r, here, :] = barrier
                    rhs_acc[r] = rhs_acc[r] + margin
                    sum_acc[r] = sum_acc[r] + scaling
                    col_rhs = margin if r == 0 else col_rhs + margin
                    col_sum_part = scaling if r == 0 else col_sum_part + scaling
                col_ref[0, here, :] += col_rhs
                col_ref[1, here, :] += col_sum_part
            for r in range(2):
                place = pl.ds(r0 + 2 * pair + r, 1)
                row_ref[0, place, :] = jnp.sum(rhs_acc[r], axis=0, keepdims=True)
                row_ref[1, place, :] = jnp.sum(sum_acc[r], axis=0, keepdims=True)

        hits = any_attack(info_ref, first_row + r0)
        pairs = BLOCK // 2

        @pl.when(hits == 0)
        def _():
            slots = (first_s, second_s)
            for j in range(ARRAYS):
                bring(0, slots[0], j)
            for pair in range(pairs):
                work(pair, slots[pair % 2], False, slots[(pair + 1) % 2] if pair + 1 < pairs else None)

        @pl.when(hits != 0)
        def _():
            def step(pair, _):
                for j in range(ARRAYS):
                    bring(pair, first_s, j)
                work(pair, first_s, True)
                return 0

            lax.fori_loop(0, pairs, step, 0)

    deep = pl.Buffered(3)
    cells = pl.BlockSpec((probs, BLOCK, sizes, inds), lambda b: (0, b, 0, 0), pipeline_mode=deep)
    shared = pl.BlockSpec((BLOCK, sizes, inds), lambda b: (b, 0, 0), pipeline_mode=deep)
    turned_cells = pl.BlockSpec((BLOCK, inds, LANES), lambda b: (b, 0, 0))
    pltpu.emit_pipeline(
        body,
        grid=(blocks,),
        in_specs=[cells, cells, cells, shared, shared],
        out_specs=[turned_cells],
    )(pos_hbm, low_hbm, high_hbm, upper_hbm, supp_hbm, barrier_hbm)
    split_halves(col_ref, keep_ref, send_ref, odd_ref)


def add_up(refs):
    values = [ref[...] for ref in refs]
    while len(values) > 1:
        values = [values[j] + values[j + 1] for j in range(0, len(values), 2)]
    return values[0]


def join_kernel(*refs):
    refs[-1][...] = add_up(refs[:-1])


def begin_kernel(count, odd_ref, *refs):
    own, other, row_diag, col_diag, row_now, col_now = refs[count:]
    both = add_up(refs[:count])
    row_diag[...] = both[1] + SHIFT_DIAG
    row_now[...] = both[0] / row_diag[...]
    half = own.shape[1]
    odd = jnp.broadcast_to(odd_ref[0:1, :] > 0, own.shape)
    halves = jnp.where(odd, other[...], own[...]), jnp.where(odd, own[...], other[...])
    for j, part in enumerate(halves):
        here = slice(j * half, (j + 1) * half)
        width = part[1] + SHIFT_DIAG
        col_diag[here, :] = width
        col_now[here, :] = part[0] / width


def row_end_kernel(*refs):
    refs[-1][...] = add_up(refs[:-2]) / refs[-2][...]


def join_halves(odd_ref, own, other, diag, out):
    half = own.shape[0]
    odd = jnp.broadcast_to(odd_ref[0:1, :] > 0, own.shape)
    out[:half, :] = jnp.where(odd, other[...], own[...]) / diag[:half, :]
    out[half:, :] = jnp.where(odd, own[...], other[...]) / diag[half:, :]


def row_kernel(scaling_ref, col_ref, out_ref):
    rows, inds, _ = scaling_ref.shape

    def step(block, _):
        here = pl.ds(pl.multiple_of(block * BLOCK, BLOCK), BLOCK)
        acc = jnp.zeros((BLOCK, 8, LANES), F32)
        for i0 in range(0, inds, 8):
            acc = acc + scaling_ref[here, i0 : i0 + 8, :] * col_ref[i0 : i0 + 8, :][None]
        out_ref[here, :] = jnp.sum(acc, axis=1)
        return 0

    lax.fori_loop(0, rows // BLOCK, step, 0)


def col_kernel(odd_ref, scaling_ref, row_ref, _, keep_ref, send_ref, out_ref):
    rows, inds, _ = scaling_ref.shape
    out_ref[...] = jnp.zeros_like(out_ref)

    def step(block, _):
        here = pl.ds(pl.multiple_of(block * BLOCK, BLOCK), BLOCK)
        row_wide = widen(row_ref[here, :])
        for i0 in range(0, inds, 8):
            out_ref[i0 : i0 + 8, :] += jnp.sum(scaling_ref[here, i0 : i0 + 8, :] * row_wide, axis=0)
        return 0

    lax.fori_loop(0, rows // BLOCK, step, 0)
    split_halves(out_ref, keep_ref, send_ref, odd_ref)


def products_kernel(iters, nreg, nind, scaling_ref, row_diag_ref, col_diag_ref, *rest):
    count = 3 * iters
    row_p, col_p = [ref[...] for ref in rest[:count]], [ref[...] for ref in rest[count : 2 * count]]
    out_ref, row_z, col_z = rest[2 * count :]
    rows, inds, _ = scaling_ref.shape
    row_zs = [row_p[3 * j] - row_p[3 * j + 1] + row_p[3 * j + 2] for j in range(iters)]
    col_zs = [col_p[3 * j] - col_p[3 * j + 1] + col_p[3 * j + 2] for j in range(iters)]
    row_z[...] = row_zs[-1]
    col_z[...] = col_zs[-1]

    def step(block, acc):
        here = pl.ds(pl.multiple_of(block * BLOCK, BLOCK), BLOCK)
        part = jnp.zeros((BLOCK, 8, LANES), F32)
        for i0 in range(0, inds, 8):
            part = part + scaling_ref[here, i0 : i0 + 8, :] * col_z[i0 : i0 + 8, :][None]
        return acc + jnp.sum(part, axis=1) * row_z[here, :]

    cross = lax.fori_loop(0, rows // BLOCK, step, jnp.zeros((BLOCK, LANES), F32))
    cross = 2.0 * jnp.sum(cross, axis=0, keepdims=True)
    row_diag, col_diag = row_diag_ref[...], col_diag_ref[...]

    def dot(j, row_v, col_v):
        row_sum = jnp.sum(row_zs[j] * row_v, axis=0, keepdims=True)
        col_sum = jnp.sum(col_zs[j] * col_v, axis=0, keepdims=True)
        return row_sum * (1.0 / nind) + col_sum * (1.0 / nreg)

    out_ref[...] = jnp.zeros_like(out_ref)
    slot = 0
    row_n, col_n = row_diag * row_p[0], col_diag * col_p[0]
    for j in range(iters):
        out_ref[slot : slot + 1, :] = dot(j, row_n, col_n)
        slot += 1
    for m in range(iters):
        last = m + 1 == iters
        row_n = row_diag * (row_zs[m] if last else row_p[3 * m] + row_p[3 * m + 3])
        col_n = col_diag * (col_zs[m] if last else col_p[3 * m] + col_p[3 * m + 3])
        for j in range(m, iters):
            product = dot(j, row_n, col_n)
            out_ref[slot : slot + 1, :] = product + cross if last else product
            slot += 1


def finish_kernel(rows, sizes, inds, probs, iters, nsum, scaling_ref, barrier_hbm, drow_ref, dcol_ref, *rest):
    count = 3 * iters
    sums, rest = rest[:nsum], rest[nsum:]
    row_p, col_p = rest[:count], rest[count : 2 * count]
    cell_hbm, row_ref, col_ref, row_add, col_add = rest[2 * count :]
    lane = lax.broadcasted_iota(jnp.int32, (LANES, LANES), 0) // sizes
    other = lax.broadcasted_iota(jnp.int32, (LANES, LANES), 1) // sizes
    same = (lane == other).astype(F32)
    total = jnp.dot(add_up(sums), same, preferred_element_type=F32, precision=lax.Precision.HIGHEST)
    g0, g1, g2, h00, h10, h20, h11, h21, h22 = [total[j : j + 1, :] for j in range(9)]
    l1, l2 = h10 / h00, h20 / h00
    d1 = h11 - l1 * h10
    t21 = h21 - l2 * h10
    m21 = t21 / d1
    d2 = h22 - l2 * h20 - m21 * t21
    y1 = g1 - l1 * g0
    y2 = g2 - l2 * g0 - m21 * y1
    c2 = y2 / d2
    c1 = y1 / d1 - m21 * c2
    c0 = g0 / h00 - l1 * c1 - l2 * c2

    def combine(refs):
        acc = None
        for j, coef in enumerate((c0, c1, c2)):
            term = coef * (refs[3 * j][...] - refs[3 * j + 1][...] + refs[3 * j + 2][...])
            acc = term if acc is None else acc + term
        return acc

    row_y = combine(row_p)
    col_y = combine(col_p)
    row_ref[...] = row_y.T
    col_ref[...] = col_y.T
    row_add[...] = row_y + drow_ref[...].T
    col_add[...] = col_y + dcol_ref[...].T

    def body(barrier_ref, cell_ref):
        r0 = pl.program_id(0) * BLOCK
        ready = None
        for r in range(BLOCK + 1):
            last = ready
            if r < BLOCK:
                ready = (col_add[...] + row_add[pl.ds(r0 + r, 1), :]) * scaling_ref[r0 + r] - barrier_ref[r]
                ready = ready.astype(jnp.bfloat16)
            if r:
                cell_ref[:, r - 1] = turned(last).astype(jnp.bfloat16).reshape(probs, sizes, inds)

    deep = pl.Buffered(4)
    cells = pl.BlockSpec((probs, BLOCK, sizes, inds), lambda b: (0, b, 0, 0))
    turned_cells = pl.BlockSpec((BLOCK, inds, LANES), lambda b: (b, 0, 0), pipeline_mode=deep)
    pltpu.emit_pipeline(body, grid=(rows // BLOCK,), in_specs=[turned_cells], out_specs=[cells])(
        barrier_hbm, cell_hbm
    )


def bits_of(count):
    return [1 << j for j in range(count.bit_length() - 1)]


def exchange(x, axis, count, bits):
    flips = [0]
    for bit in bits:
        flips = flips + [flip | bit for flip in flips]
    return [x] + [lax.ppermute(x, axis, [(j, j ^ flip) for j in range(count)]) for flip in flips[1:]]


def vmem_call(kernel, outs, name, scratch=(), cost=None):
    def call(*args):
        return pl.pallas_call(
            kernel,
            out_shape=outs,
            in_specs=[VMEM_SPEC] * len(args),
            out_specs=[VMEM_SPEC] * len(outs),
            scratch_shapes=list(scratch),
            compiler_params=params(),
            cost_estimate=cost,
            name=name,
        )(*args)

    return call


def join(parts):
    return vmem_call(join_kernel, [shape(*parts[0].shape)], "join")(*parts)[0]


def row_sum(x, nind):
    parts = [x]
    for bit in bits_of(nind):
        if len(parts) > 1:
            x = join(parts)
        parts = exchange(x, "industry", nind, [bit])
    return parts


def col_sum(keep, send, nreg):
    (arrived,) = exchange(send, "region", nreg, [1])[1:]
    x = join([keep, arrived])
    bits = bits_of(nreg)[1:]
    for j in range(0, len(bits), 2):
        x = join(exchange(x, "region", nreg, bits[j : j + 2]))
    return exchange(x, "region", nreg, [1])


def local(
    nreg, nind, iters,
    position, dual_lower, dual_upper, upper_bound, suppressed,
    attack_region, attack_column, dual_row, dual_col,
):
    probs, rows, sizes, inds = position.shape
    my_reg, my_ind = lax.axis_index("region"), lax.axis_index("industry")
    info = jnp.concatenate([jnp.stack([my_reg, my_ind]).astype(jnp.int32), attack_region, attack_column])
    odd = jnp.broadcast_to(lax.rem(my_reg, 2).astype(F32), (8, LANES))
    drow = dual_row.transpose(0, 2, 1).reshape(LANES, rows)
    dcol = dual_col.reshape(LANES, inds)
    half = inds // 2

    def in_hbm(x):
        return pltpu.with_memory_space_constraint(x, pltpu.HBM)

    def keep(x):
        return pltpu.with_memory_space_constraint(x, pltpu.VMEM)

    position, dual_lower, dual_upper = map(in_hbm, (position, dual_lower, dual_upper))
    upper_bound, suppressed = map(in_hbm, (upper_bound, suppressed))
    scaling, barrier, row_both, col_keep, col_send = pl.pallas_call(
        functools.partial(prepare_kernel, rows, sizes, inds, probs, nind),
        out_shape=[
            pltpu.VMEM((rows, inds, LANES), F32),
            shape(rows, inds, LANES),
            shape(2, rows, LANES),
            shape(2, half, LANES),
            shape(2, half, LANES),
        ],
        in_specs=[SMEM_SPEC, VMEM_SPEC] + [ANY_SPEC] * 5 + [VMEM_SPEC] * 2,
        out_specs=[VMEM_SPEC, ANY_SPEC] + [VMEM_SPEC] * 3,
        scratch_shapes=[
            pltpu.VMEM((ARRAYS, inds, 2 * LANES), F32),
            pltpu.VMEM((ARRAYS, inds, 2 * LANES), F32),
            pltpu.VMEM((rows, LANES), F32),
            pltpu.VMEM((inds, LANES), F32),
            pltpu.VMEM((2, inds, LANES), F32),
        ],
        compiler_params=params(),
        name="prepare",
    )(info, odd, position, dual_lower, dual_upper, upper_bound, suppressed, drow, dcol)
    scaling = keep(scaling)
    barrier = in_hbm(barrier)
    cells = rows * inds * LANES
    cost = pl.CostEstimate(flops=2 * cells, bytes_accessed=4 * cells, transcendentals=0)
    margins = [shape(rows, LANES), shape(inds, LANES)]
    row_parts = row_sum(row_both, nind)
    col_halves = col_sum(col_keep, col_send, nreg)
    kernel = functools.partial(begin_kernel, len(row_parts))
    row_diag, col_diag, row_now, col_now = vmem_call(kernel, margins * 2, "begin")(
        odd, *row_parts, *col_halves
    )
    row_p, col_p = [row_now], [col_now]
    for _ in range(3 * iters - 1):
        (row_out,) = vmem_call(row_kernel, margins[:1], "row_sweep", cost=cost)(scaling, col_p[-1])
        col_keep, col_send = vmem_call(
            col_kernel, [shape(half, LANES)] * 2, "col_sweep", [pltpu.VMEM((inds, LANES), F32)], cost
        )(odd, scaling, row_p[-1], row_out)
        row_parts = row_sum(row_out, nind)
        col_halves = col_sum(col_keep, col_send, nreg)
        row_p += vmem_call(row_end_kernel, margins[:1], "row_end")(*row_parts, row_diag)
        col_p += vmem_call(join_halves, margins[1:], "col_end")(odd, *col_halves, col_diag)
    kernel = functools.partial(products_kernel, iters, nreg, nind)
    scratch = [pltpu.VMEM((rows, LANES), F32), pltpu.VMEM((inds, LANES), F32)]
    (part,) = vmem_call(kernel, [shape(16, LANES)], "products", scratch)(
        scaling, row_diag, col_diag, *row_p, *col_p
    )
    bits = bits_of(nreg)
    part = join(exchange(part, "region", nreg, bits[:1]))
    for j in range(1, len(bits), 2):
        part = join(exchange(part, "region", nreg, bits[j : j + 2]))
    bits = bits_of(nind)
    for bit in bits[2:]:
        part = join(exchange(part, "industry", nind, [bit]))
    sums = exchange(part, "industry", nind, bits[:2])
    cell, row_y, col_y = pl.pallas_call(
        functools.partial(finish_kernel, rows, sizes, inds, probs, iters, len(sums)),
        out_shape=[
            jax.ShapeDtypeStruct((probs, rows, sizes, inds), jnp.bfloat16),
            shape(LANES, rows),
            shape(LANES, inds),
        ],
        in_specs=[VMEM_SPEC, ANY_SPEC] + [VMEM_SPEC] * (2 + len(sums) + 6 * iters),
        out_specs=[ANY_SPEC, VMEM_SPEC, VMEM_SPEC],
        scratch_shapes=[pltpu.VMEM((rows, LANES), F32), pltpu.VMEM((inds, LANES), F32)],
        compiler_params=params(),
        name="finish",
    )(scaling, barrier, drow, dcol, *sums, *row_p, *col_p)
    row_step = row_y.reshape(probs, sizes, rows).transpose(0, 2, 1)
    col_step = col_y.reshape(probs, sizes, inds)
    return cell, row_step, col_step


def solution(mesh):
    nreg, nind = mesh.shape["region"], mesh.shape["industry"]
    cells = P(None, "region", None, "industry")
    table = P("region", None, "industry")
    row, col = P(None, "region", None), P(None, None, "industry")
    return jax.shard_map(
        functools.partial(local, nreg, nind, 3),
        mesh=mesh,
        in_specs=(cells, cells, cells, table, table, P(), P(), row, col),
        out_specs=(cells, row, col),
        check_vma=False,
    )
```

```python
import functools

import jax
import jax.numpy as jnp
from jax import lax
from jax.experimental import pallas as pl
from jax.experimental.pallas import tpu as pltpu
from jax.sharding import PartitionSpec as P

WEIGHT_ATTACK = 8.0
SHIFT_DIAG = 1.0
BLOCK = 8
LANES = 128
VMEM_MIB = 12
VMEM_SPEC = pl.BlockSpec(memory_space=pltpu.VMEM)
SMEM_SPEC = pl.BlockSpec(memory_space=pltpu.SMEM)
ANY_SPEC = pl.BlockSpec(memory_space=pl.ANY)
F32 = jnp.float32


def shape(*dims):
    return jax.ShapeDtypeStruct(dims, F32)


def params():
    return pltpu.CompilerParams(vmem_limit_bytes=VMEM_MIB * 1024 * 1024)


def inverse(x):
    rough = pl.reciprocal(x, approx=True)
    return rough * (2.0 - x * rough)


def widen(rows):
    return jnp.broadcast_to(rows[:, None, :], (BLOCK, 8, LANES))


def turned(x, eye_ref):
    return lax.dot_general(eye_ref[...], x, (((1,), (1,)), ((), ())), preferred_element_type=F32)


def identity(size):
    row = lax.broadcasted_iota(jnp.int32, (size, size), 0)
    return (row == lax.broadcasted_iota(jnp.int32, (size, size), 1)).astype(F32).astype(jnp.bfloat16)


def any_attack(info_ref, first_row):
    hits = jnp.int32(0)
    for k in range((info_ref.shape[0] - 2) // 2):
        offset = info_ref[2 + k] - first_row
        hits = hits + jnp.where((offset >= 0) & (offset < BLOCK), 1, 0)
    return hits


def split_halves(full, keep_ref, send_ref, odd_ref):
    half = full.shape[-2] // 2
    odd = jnp.broadcast_to(odd_ref[0:1, :] > 0, keep_ref.shape)
    first, second = full[..., :half, :], full[..., half:, :]
    keep_ref[...] = jnp.where(odd, second, first)
    send_ref[...] = jnp.where(odd, first, second)


def prepare_kernel(
    rows, sizes, inds, probs, nind,
    info_ref, odd_ref, pos_hbm, low_hbm, high_hbm, upper_hbm, supp_hbm, drow_ref, dcol_ref,
    scaling_ref, barrier_hbm, row_ref, keep_ref, send_ref,
    first_s, second_s, drow_t, dcol_t, col_ref, eye_ref,
):
    blocks = rows // BLOCK
    first_row = info_ref[0] * rows
    first_ind = info_ref[1] * inds
    col_ref[...] = jnp.zeros_like(col_ref)
    eye_ref[...] = identity(inds)
    drow_t[...] = drow_ref[...].T
    dcol_t[...] = dcol_ref[...].T

    def body(pos_ref, low_ref, high_ref, upper_ref, supp_ref, barrier_ref):
        r0 = pl.multiple_of(pl.program_id(0) * BLOCK, BLOCK)

        def bring(pair, slot):
            for j, ref in enumerate((pos_ref, low_ref, high_ref)):
                both = [ref[:, 2 * pair + r].reshape(LANES, inds) for r in range(2)]
                slot[j] = turned(jnp.concatenate(both, axis=0), eye_ref)
            for j, ref in enumerate((upper_ref, supp_ref)):
                both = []
                for r in range(2):
                    one = ref[2 * pair + r].astype(F32).astype(jnp.bfloat16)
                    both += [one] * probs
                slot[3 + j] = turned(jnp.concatenate(both, axis=0), eye_ref)

        def work(pair, slot, attacked):
            rhs_acc = [jnp.zeros((8, LANES), F32)] * 2
            sum_acc = [jnp.zeros((8, LANES), F32)] * 2
            drow = [
                jnp.broadcast_to(drow_t[pl.ds(r0 + 2 * pair + r, 1), :], (8, LANES)) for r in range(2)
            ]
            for i0 in range(0, inds, 8):
                here = slice(i0, i0 + 8)
                dcol = dcol_t[here, :]
                col_rhs = col_sum_part = None
                for r in range(2):
                    lanes = slice(r * LANES, (r + 1) * LANES)
                    upper = slot[3, here, lanes]
                    active = slot[4, here, lanes]
                    if attacked:
                        lane = lax.broadcasted_iota(jnp.int32, (8, LANES), 1)
                        column = lax.rem(lane, sizes) * (inds * nind) + first_ind + i0
                        column = column + lax.broadcasted_iota(jnp.int32, (8, LANES), 0)
                        row = first_row + r0 + 2 * pair + r
                        goal = jnp.full((8, LANES), -1, jnp.int32)
                        for k in range(probs):
                            mine = jnp.where(info_ref[2 + k] == row, info_ref[2 + probs + k], -1)
                            goal = jnp.where(lane // sizes == k, mine, goal)
                        hit = goal == column
                        active = jnp.where(hit, jnp.ones_like(active), active)
                    value = slot[0, here, lanes] * upper
                    slack = upper - value
                    den = slot[1, here, lanes] * slack + slot[2, here, lanes] * value
                    ratio = active * inverse(den)
                    scaling = value * slack * ratio
                    middle = 0.5 * upper - value
                    barrier = middle * ratio
                    if attacked:
                        barrier = barrier + jnp.where(hit, WEIGHT_ATTACK * scaling, jnp.zeros_like(scaling))
                    margin = middle * active + barrier - scaling * (drow[r] + dcol)
                    scaling_ref[r0 + 2 * pair + r, here, :] = scaling
                    barrier_ref[2 * pair + r, here, :] = barrier
                    rhs_acc[r] = rhs_acc[r] + margin
                    sum_acc[r] = sum_acc[r] + scaling
                    col_rhs = margin if r == 0 else col_rhs + margin
                    col_sum_part = scaling if r == 0 else col_sum_part + scaling
                col_ref[0, here, :] += col_rhs
                col_ref[1, here, :] += col_sum_part
            for r in range(2):
                place = pl.ds(r0 + 2 * pair + r, 1)
                row_ref[0, place, :] = jnp.sum(rhs_acc[r], axis=0, keepdims=True)
                row_ref[1, place, :] = jnp.sum(sum_acc[r], axis=0, keepdims=True)

        hits = any_attack(info_ref, first_row + r0)
        pairs = BLOCK // 2

        @pl.when(hits == 0)
        def _():
            slots = (first_s, second_s)
            bring(0, slots[0])
            for pair in range(pairs):
                if pair + 1 < pairs:
                    bring(pair + 1, slots[(pair + 1) % 2])
                work(pair, slots[pair % 2], False)

        @pl.when(hits != 0)
        def _():
            def step(pair, _):
                bring(pair, first_s)
                work(pair, first_s, True)
                return 0

            lax.fori_loop(0, pairs, step, 0)

    deep = pl.Buffered(3)
    cells = pl.BlockSpec((probs, BLOCK, sizes, inds), lambda b: (0, b, 0, 0), pipeline_mode=deep)
    shared = pl.BlockSpec((BLOCK, sizes, inds), lambda b: (b, 0, 0), pipeline_mode=deep)
    turned_cells = pl.BlockSpec((BLOCK, inds, LANES), lambda b: (b, 0, 0))
    pltpu.emit_pipeline(
        body,
        grid=(blocks,),
        in_specs=[cells, cells, cells, shared, shared],
        out_specs=[turned_cells],
    )(pos_hbm, low_hbm, high_hbm, upper_hbm, supp_hbm, barrier_hbm)
    split_halves(col_ref, keep_ref, send_ref, odd_ref)


def add_up(refs):
    values = [ref[...] for ref in refs]
    while len(values) > 1:
        values = [values[j] + values[j + 1] for j in range(0, len(values), 2)]
    return values[0]


def join_kernel(*refs):
    refs[-1][...] = add_up(refs[:-1])


def begin_kernel(count, odd_ref, *refs):
    own, other, row_diag, col_diag, row_now, col_now = refs[count:]
    both = add_up(refs[:count])
    row_diag[...] = both[1] + SHIFT_DIAG
    row_now[...] = both[0] / row_diag[...]
    half = own.shape[1]
    odd = jnp.broadcast_to(odd_ref[0:1, :] > 0, own.shape)
    halves = jnp.where(odd, other[...], own[...]), jnp.where(odd, own[...], other[...])
    for j, part in enumerate(halves):
        here = slice(j * half, (j + 1) * half)
        width = part[1] + SHIFT_DIAG
        col_diag[here, :] = width
        col_now[here, :] = part[0] / width


def row_end_kernel(*refs):
    refs[-1][...] = add_up(refs[:-2]) / refs[-2][...]


def join_halves(odd_ref, own, other, diag, out):
    half = own.shape[0]
    odd = jnp.broadcast_to(odd_ref[0:1, :] > 0, own.shape)
    out[:half, :] = jnp.where(odd, other[...], own[...]) / diag[:half, :]
    out[half:, :] = jnp.where(odd, own[...], other[...]) / diag[half:, :]


def row_kernel(scaling_ref, col_ref, out_ref):
    rows, inds, _ = scaling_ref.shape

    def step(block, _):
        here = pl.ds(pl.multiple_of(block * BLOCK, BLOCK), BLOCK)
        acc = jnp.zeros((BLOCK, 8, LANES), F32)
        for i0 in range(0, inds, 8):
            acc = acc + scaling_ref[here, i0 : i0 + 8, :] * col_ref[i0 : i0 + 8, :][None]
        out_ref[here, :] = jnp.sum(acc, axis=1)
        return 0

    lax.fori_loop(0, rows // BLOCK, step, 0)


def col_kernel(odd_ref, scaling_ref, row_ref, _, keep_ref, send_ref, out_ref):
    rows, inds, _ = scaling_ref.shape
    out_ref[...] = jnp.zeros_like(out_ref)

    def step(block, _):
        here = pl.ds(pl.multiple_of(block * BLOCK, BLOCK), BLOCK)
        row_wide = widen(row_ref[here, :])
        for i0 in range(0, inds, 8):
            out_ref[i0 : i0 + 8, :] += jnp.sum(scaling_ref[here, i0 : i0 + 8, :] * row_wide, axis=0)
        return 0

    lax.fori_loop(0, rows // BLOCK, step, 0)
    split_halves(out_ref, keep_ref, send_ref, odd_ref)


def products_kernel(iters, nreg, nind, scaling_ref, row_diag_ref, col_diag_ref, *rest):
    count = 3 * iters
    row_p, col_p = [ref[...] for ref in rest[:count]], [ref[...] for ref in rest[count : 2 * count]]
    out_ref, row_z, col_z = rest[2 * count :]
    rows, inds, _ = scaling_ref.shape
    row_zs = [row_p[3 * j] - row_p[3 * j + 1] + row_p[3 * j + 2] for j in range(iters)]
    col_zs = [col_p[3 * j] - col_p[3 * j + 1] + col_p[3 * j + 2] for j in range(iters)]
    row_z[...] = row_zs[-1]
    col_z[...] = col_zs[-1]

    def step(block, acc):
        here = pl.ds(pl.multiple_of(block * BLOCK, BLOCK), BLOCK)
        part = jnp.zeros((BLOCK, 8, LANES), F32)
        for i0 in range(0, inds, 8):
            part = part + scaling_ref[here, i0 : i0 + 8, :] * col_z[i0 : i0 + 8, :][None]
        return acc + jnp.sum(part, axis=1) * row_z[here, :]

    cross = lax.fori_loop(0, rows // BLOCK, step, jnp.zeros((BLOCK, LANES), F32))
    cross = 2.0 * jnp.sum(cross, axis=0, keepdims=True)
    row_diag, col_diag = row_diag_ref[...], col_diag_ref[...]

    def dot(j, row_v, col_v):
        row_sum = jnp.sum(row_zs[j] * row_v, axis=0, keepdims=True)
        col_sum = jnp.sum(col_zs[j] * col_v, axis=0, keepdims=True)
        return row_sum * (1.0 / nind) + col_sum * (1.0 / nreg)

    out_ref[...] = jnp.zeros_like(out_ref)
    slot = 0
    row_n, col_n = row_diag * row_p[0], col_diag * col_p[0]
    for j in range(iters):
        out_ref[slot : slot + 1, :] = dot(j, row_n, col_n)
        slot += 1
    for m in range(iters):
        last = m + 1 == iters
        row_n = row_diag * (row_zs[m] if last else row_p[3 * m] + row_p[3 * m + 3])
        col_n = col_diag * (col_zs[m] if last else col_p[3 * m] + col_p[3 * m + 3])
        for j in range(m, iters):
            product = dot(j, row_n, col_n)
            out_ref[slot : slot + 1, :] = product + cross if last else product
            slot += 1


def finish_kernel(rows, sizes, inds, probs, iters, nsum, scaling_ref, barrier_hbm, drow_ref, dcol_ref, *rest):
    count = 3 * iters
    sums, rest = rest[:nsum], rest[nsum:]
    row_p, col_p = rest[:count], rest[count : 2 * count]
    cell_hbm, row_ref, col_ref, row_add, col_add, eye_ref = rest[2 * count :]
    eye_ref[...] = identity(LANES)
    lane = lax.broadcasted_iota(jnp.int32, (LANES, LANES), 0) // sizes
    other = lax.broadcasted_iota(jnp.int32, (LANES, LANES), 1) // sizes
    same = (lane == other).astype(F32)
    total = jnp.dot(add_up(sums), same, preferred_element_type=F32, precision=lax.Precision.HIGHEST)
    g0, g1, g2, h00, h10, h20, h11, h21, h22 = [total[j : j + 1, :] for j in range(9)]
    l1, l2 = h10 / h00, h20 / h00
    d1 = h11 - l1 * h10
    t21 = h21 - l2 * h10
    m21 = t21 / d1
    d2 = h22 - l2 * h20 - m21 * t21
    y1 = g1 - l1 * g0
    y2 = g2 - l2 * g0 - m21 * y1
    c2 = y2 / d2
    c1 = y1 / d1 - m21 * c2
    c0 = g0 / h00 - l1 * c1 - l2 * c2

    def combine(refs):
        acc = None
        for j, coef in enumerate((c0, c1, c2)):
            term = coef * (refs[3 * j][...] - refs[3 * j + 1][...] + refs[3 * j + 2][...])
            acc = term if acc is None else acc + term
        return acc

    row_y = combine(row_p)
    col_y = combine(col_p)
    row_ref[...] = row_y.T
    col_ref[...] = col_y.T
    row_add[...] = row_y + drow_ref[...].T
    col_add[...] = col_y + dcol_ref[...].T

    def body(barrier_ref, cell_ref):
        r0 = pl.program_id(0) * BLOCK
        for r in range(BLOCK):
            cell = (col_add[...] + row_add[pl.ds(r0 + r, 1), :]) * scaling_ref[r0 + r] - barrier_ref[r]
            cell = turned(cell.astype(jnp.bfloat16), eye_ref)
            cell_ref[:, r] = cell.astype(jnp.bfloat16).reshape(probs, sizes, inds)

    deep = pl.Buffered(4)
    cells = pl.BlockSpec((probs, BLOCK, sizes, inds), lambda b: (0, b, 0, 0))
    turned_cells = pl.BlockSpec((BLOCK, inds, LANES), lambda b: (b, 0, 0), pipeline_mode=deep)
    pltpu.emit_pipeline(body, grid=(rows // BLOCK,), in_specs=[turned_cells], out_specs=[cells])(
        barrier_hbm, cell_hbm
    )


def bits_of(count):
    return [1 << j for j in range(count.bit_length() - 1)]


def exchange(x, axis, count, bits):
    flips = [0]
    for bit in bits:
        flips = flips + [flip | bit for flip in flips]
    return [x] + [lax.ppermute(x, axis, [(j, j ^ flip) for j in range(count)]) for flip in flips[1:]]


def vmem_call(kernel, outs, name, scratch=(), cost=None):
    def call(*args):
        return pl.pallas_call(
            kernel,
            out_shape=outs,
            in_specs=[VMEM_SPEC] * len(args),
            out_specs=[VMEM_SPEC] * len(outs),
            scratch_shapes=list(scratch),
            compiler_params=params(),
            cost_estimate=cost,
            name=name,
        )(*args)

    return call


def join(parts):
    return vmem_call(join_kernel, [shape(*parts[0].shape)], "join")(*parts)[0]


def row_sum(x, nind):
    parts = [x]
    for bit in bits_of(nind):
        if len(parts) > 1:
            x = join(parts)
        parts = exchange(x, "industry", nind, [bit])
    return parts


def col_sum(keep, send, nreg):
    (arrived,) = exchange(send, "region", nreg, [1])[1:]
    x = join([keep, arrived])
    bits = bits_of(nreg)[1:]
    for j in range(0, len(bits), 2):
        x = join(exchange(x, "region", nreg, bits[j : j + 2]))
    return exchange(x, "region", nreg, [1])


def local(
    nreg, nind, iters,
    position, dual_lower, dual_upper, upper_bound, suppressed,
    attack_region, attack_column, dual_row, dual_col,
):
    probs, rows, sizes, inds = position.shape
    my_reg, my_ind = lax.axis_index("region"), lax.axis_index("industry")
    info = jnp.concatenate([jnp.stack([my_reg, my_ind]).astype(jnp.int32), attack_region, attack_column])
    odd = jnp.broadcast_to(lax.rem(my_reg, 2).astype(F32), (8, LANES))
    drow = dual_row.transpose(0, 2, 1).reshape(LANES, rows)
    dcol = dual_col.reshape(LANES, inds)
    half = inds // 2

    def in_hbm(x):
        return pltpu.with_memory_space_constraint(x, pltpu.HBM)

    def keep(x):
        return pltpu.with_memory_space_constraint(x, pltpu.VMEM)

    position, dual_lower, dual_upper = map(in_hbm, (position, dual_lower, dual_upper))
    upper_bound, suppressed = map(in_hbm, (upper_bound, suppressed))
    scaling, barrier, row_both, col_keep, col_send = pl.pallas_call(
        functools.partial(prepare_kernel, rows, sizes, inds, probs, nind),
        out_shape=[
            pltpu.VMEM((rows, inds, LANES), F32),
            shape(rows, inds, LANES),
            shape(2, rows, LANES),
            shape(2, half, LANES),
            shape(2, half, LANES),
        ],
        in_specs=[SMEM_SPEC, VMEM_SPEC] + [ANY_SPEC] * 5 + [VMEM_SPEC] * 2,
        out_specs=[VMEM_SPEC, ANY_SPEC] + [VMEM_SPEC] * 3,
        scratch_shapes=[
            pltpu.VMEM((5, inds, 2 * LANES), F32),
            pltpu.VMEM((5, inds, 2 * LANES), F32),
            pltpu.VMEM((rows, LANES), F32),
            pltpu.VMEM((inds, LANES), F32),
            pltpu.VMEM((2, inds, LANES), F32),
            pltpu.VMEM((inds, inds), jnp.bfloat16),
        ],
        compiler_params=params(),
        name="prepare",
    )(info, odd, position, dual_lower, dual_upper, upper_bound, suppressed, drow, dcol)
    scaling = keep(scaling)
    barrier = in_hbm(barrier)
    cells = rows * inds * LANES
    cost = pl.CostEstimate(flops=2 * cells, bytes_accessed=4 * cells, transcendentals=0)
    margins = [shape(rows, LANES), shape(inds, LANES)]
    row_parts = row_sum(row_both, nind)
    col_halves = col_sum(col_keep, col_send, nreg)
    kernel = functools.partial(begin_kernel, len(row_parts))
    row_diag, col_diag, row_now, col_now = vmem_call(kernel, margins * 2, "begin")(
        odd, *row_parts, *col_halves
    )
    row_p, col_p = [row_now], [col_now]
    for _ in range(3 * iters - 1):
        (row_out,) = vmem_call(row_kernel, margins[:1], "row_sweep", cost=cost)(scaling, col_p[-1])
        col_keep, col_send = vmem_call(
            col_kernel, [shape(half, LANES)] * 2, "col_sweep", [pltpu.VMEM((inds, LANES), F32)], cost
        )(odd, scaling, row_p[-1], row_out)
        row_parts = row_sum(row_out, nind)
        col_halves = col_sum(col_keep, col_send, nreg)
        row_p += vmem_call(row_end_kernel, margins[:1], "row_end")(*row_parts, row_diag)
        col_p += vmem_call(join_halves, margins[1:], "col_end")(odd, *col_halves, col_diag)
    kernel = functools.partial(products_kernel, iters, nreg, nind)
    scratch = [pltpu.VMEM((rows, LANES), F32), pltpu.VMEM((inds, LANES), F32)]
    (part,) = vmem_call(kernel, [shape(16, LANES)], "products", scratch)(
        scaling, row_diag, col_diag, *row_p, *col_p
    )
    bits = bits_of(nreg)
    part = join(exchange(part, "region", nreg, bits[:1]))
    for j in range(1, len(bits), 2):
        part = join(exchange(part, "region", nreg, bits[j : j + 2]))
    bits = bits_of(nind)
    for bit in bits[2:]:
        part = join(exchange(part, "industry", nind, [bit]))
    sums = exchange(part, "industry", nind, bits[:2])
    cell, row_y, col_y = pl.pallas_call(
        functools.partial(finish_kernel, rows, sizes, inds, probs, iters, len(sums)),
        out_shape=[
            jax.ShapeDtypeStruct((probs, rows, sizes, inds), jnp.bfloat16),
            shape(LANES, rows),
            shape(LANES, inds),
        ],
        in_specs=[VMEM_SPEC, ANY_SPEC] + [VMEM_SPEC] * (2 + len(sums) + 6 * iters),
        out_specs=[ANY_SPEC, VMEM_SPEC, VMEM_SPEC],
        scratch_shapes=[
            pltpu.VMEM((rows, LANES), F32),
            pltpu.VMEM((inds, LANES), F32),
            pltpu.VMEM((LANES, LANES), jnp.bfloat16),
        ],
        compiler_params=params(),
        name="finish",
    )(scaling, barrier, drow, dcol, *sums, *row_p, *col_p)
    row_step = row_y.reshape(probs, sizes, rows).transpose(0, 2, 1)
    col_step = col_y.reshape(probs, sizes, inds)
    return cell, row_step, col_step


def solution(mesh):
    nreg, nind = mesh.shape["region"], mesh.shape["industry"]
    cells = P(None, "region", None, "industry")
    table = P("region", None, "industry")
    row, col = P(None, "region", None), P(None, None, "industry")
    return jax.shard_map(
        functools.partial(local, nreg, nind, 3),
        mesh=mesh,
        in_specs=(cells, cells, cells, table, table, P(), P(), row, col),
        out_specs=(cells, row, col),
        check_vma=False,
    )
```
